128 devices in a mesh: dap: 64 (over y_lo, x, z, core), rep: 2 (over y_hi).
Axes of the slice: x: 4, y: 4 (y_hi: 2, y_lo: 2; y = y_hi * 2 + y_lo), z: 4, core: 2. Of those that a mesh axis runs over, the one named last changes fastest.
Arguments:
- pair_map: bfloat16 [1024, 1024, 128], P('dap'), may hold values from -6 to 6
- residue_mask: int32 [1024], replicated, may hold values from 0 to 1, as said below
- gain_start: float32 [128], replicated, may hold values from 0.25 to 1.75
- proj_start: bfloat16 [4, 128, 128], P(None, None, 'rep'), may hold values from -4 to 4
- bias_start: bfloat16 [128, 4], P(None, 'rep'), may hold values from -0.5 to 0.5
- out_start: bfloat16 [128, 128], replicated, may hold values from -3 to 3
- gain_end: float32 [128], replicated, may hold values from 0.25 to 1.75
- proj_end: bfloat16 [4, 128, 128], P(None, None, 'rep'), may hold values from -4 to 4
- bias_end: bfloat16 [128, 4], P(None, 'rep'), may hold values from -0.5 to 0.5
- out_end: bfloat16 [128, 128], replicated, may hold values from -3 to 3
Outputs:
- turned_map: bfloat16 [1024, 1024, 128], P('dap')
The draws below stay inside these ranges and needn't reach their ends.
Inputs may be any that keep to these rules, and one draw needn't show every extreme that they name: residue_mask is 1 on the first L residues and 0 on the others, for some L from 512 to 1023.
All inputs are finite; a program needn't handle non-finite values.
Results may differ from the reference program's by a relative error of at most 0.008.
The reference program's roundings to bfloat16 on the way count: a program that leaves them out, or rounds other values in their place, can miss the bound.
Values may be sent and summed in bfloat16 or wider, within the bound.
A program may use at most 128 MiB of HBM per device.

```python
import jax
import jax.numpy as jnp
from jax import lax

C = 128
H = 4
DH = 32
N = 1024
HD = 128


def base_entries(key):
    return jnp.clip(jax.random.normal(key, (4, C, H * DH), jnp.float32), -3.0, 3.0) * C ** (-0.5)


def draw_proj_start(key, part):
    key = jax.random.fold_in(key, 11)
    entries = base_entries(key)
    return entries.astype(jnp.bfloat16)


def draw_proj_end(key, part):
    key = jax.random.fold_in(key, 23)
    entries = base_entries(key)
    return entries.astype(jnp.bfloat16)


def draw_residue_mask(key, part):
    key = jax.random.fold_in(key, 5)
    length = jax.random.randint(key, (), N // 2, N)
    return (jnp.arange(N) < length).astype(jnp.int32)


def levels(stream_key, dims, cuts, low, top_value):
    def one(position, blocks):
        heights = jax.random.uniform(jax.random.fold_in(jax.random.fold_in(stream_key, 6), position), (blocks,), jnp.float32, low / len(cuts), top_value / len(cuts))
        return jnp.repeat(jnp.exp(heights), dims[position] // blocks).reshape((-1,) + (1,) * (len(dims) - position - 1))

    level = one(*cuts[0])
    for cut in cuts[1:]:
        level = level * one(*cut)
    return level


def scatter_about(key, shape, scale, reach, cuts=(), dtype=jnp.bfloat16):
    result = jax.random.normal(key, shape, jnp.float32) * scale
    if len(cuts) > 0:
        result = levels(key, shape, cuts, -0.22, 0.18) * result
    return jnp.clip(result, min=-reach, max=reach).astype(dtype)


def setup_inputs(seed: int = 0) -> dict:
    seeds = jax.random.split(jax.random.key(seed), 11)
    return {
        "pair_map": scatter_about(seeds[0], (N, N, C), 1.0, 6.0, ((0, 64),)),
        "residue_mask": draw_residue_mask(jax.random.fold_in(seeds[10], 71), 0),
        "gain_start": jnp.clip(1.0 + 0.15 * jax.random.normal(seeds[2], (C,), jnp.float32), 0.25, 1.75),
        "proj_start": draw_proj_start(jax.random.fold_in(seeds[10], 71), 0),
        "bias_start": scatter_about(seeds[4], (C, H), C ** -0.5, 0.5, ((1, 2),)),
        "out_start": scatter_about(seeds[5], (HD, C), 0.5, 3.0),
        "gain_end": jnp.clip(1.0 + 0.15 * jax.random.normal(seeds[6], (C,), jnp.float32), 0.25, 1.75),
        "proj_end": draw_proj_end(jax.random.fold_in(seeds[10], 71), 0),
        "bias_end": scatter_about(seeds[8], (C, H), C ** -0.5, 0.5, ((1, 2),)),
        "out_end": scatter_about(seeds[9], (HD, C), 0.5, 3.0),
    }


epsilon = 1e-05

def normalize(values_in, gain):
    floats = values_in.astype(jnp.float32)
    center = lax.optimization_barrier(jnp.mean(floats, axis=-1, keepdims=True))
    spread = lax.optimization_barrier(jnp.mean((floats - center) ** 2, axis=-1, keepdims=True))
    return ((floats - center) * lax.rsqrt(spread + epsilon) * gain).astype(jnp.bfloat16)

def module(pair_in, residue_mask, gain, projection, bias_weight, out_weight):
    length = pair_in.shape[0]
    heads_all = bias_weight.shape[1]
    width = projection.shape[2]
    head_dim = width // heads_all
    key_valid = residue_mask == 1

    def plane_row(row_in):
        normed = normalize(row_in, gain)
        return jnp.dot(normed, bias_weight, preferred_element_type=jnp.float32).astype(jnp.bfloat16)
    plane = jnp.transpose(lax.map(plane_row, pair_in), (2, 0, 1))
    proj_float = projection.astype(jnp.float32)

    def one_row(inputs):
        row_in, row_flag = inputs
        normed = normalize(row_in, gain).astype(jnp.float32)
        parts = jnp.einsum('bc,fch->fbh', normed, proj_float)
        queries = (parts[0] * head_dim ** (-0.5)).astype(jnp.bfloat16).astype(jnp.float32)
        key_proj = parts[1].astype(jnp.bfloat16).astype(jnp.float32)
        value_proj = parts[2].astype(jnp.bfloat16).astype(jnp.float32)
        gate_vals = jax.nn.sigmoid(parts[3])
        query_heads = queries.reshape(length, heads_all, head_dim)
        key_heads = key_proj.reshape(length, heads_all, head_dim)
        value_heads = value_proj.reshape(length, heads_all, head_dim)
        scores = jnp.einsum('qhd,khd->hqk', query_heads, key_heads) + plane.astype(jnp.float32)
        scores = jnp.where(key_valid[None, None, :], scores, -1000000000.0)
        highest = lax.optimization_barrier(jnp.max(scores, axis=-1, keepdims=True))
        expo = jnp.exp(scores - highest)
        attn = (expo / lax.optimization_barrier(jnp.sum(expo, axis=-1, keepdims=True))).astype(jnp.bfloat16).astype(jnp.float32)
        outputs = jnp.einsum('hqk,khd->qhd', attn, value_heads).reshape(length, width)
        gated = (outputs * gate_vals).astype(jnp.bfloat16)
        update = jnp.dot(gated, out_weight, preferred_element_type=jnp.float32)
        keep = (row_flag * residue_mask).astype(jnp.float32)[:, None]
        return (row_in.astype(jnp.float32) + update * keep).astype(jnp.bfloat16)
    return lax.map(one_row, (pair_in, residue_mask))

def reference(pair_map, residue_mask, gain_start, proj_start, bias_start, out_start, gain_end, proj_end, bias_end, out_end):
    mid_map = module(pair_map, residue_mask, gain_start, proj_start, bias_start, out_start)
    turned = jnp.transpose(mid_map, (1, 0, 2))
    return module(turned, residue_mask, gain_end, proj_end, bias_end, out_end)
```

```python
import functools, math
import jax, jax.numpy as jnp
from jax import lax
from jax.experimental import pallas as pl
from jax.experimental.pallas import tpu as pltpu
from jax.sharding import PartitionSpec as P

EPS=1e-5
LOG2E=math.log2(math.e)

def attn_kernel(L_ref, pair_ref, gain_ref, w_ref, plane_ref, outw_ref, out_ref,
                bias_ref, q_ref, k_ref, va_ref, g_ref, *, QB, KG, n, heads, dh):
    i = pl.program_id(0)
    L = L_ref[0]
    row0 = L_ref[1]
    C = pair_ref.shape[2]
    W = heads*dh
    blocks, hr, _ = plane_ref.shape
    rows = hr//heads
    lane = lax.broadcasted_iota(jnp.int32, (1, W), 1)//dh

    @pl.when(i == 0)
    def _():
        valid = lax.broadcasted_iota(jnp.int32, (1, n), 1) < L
        def prep(b, c):
            piece = plane_ref[b].astype(jnp.float32)
            piece = jnp.where(valid, piece*LOG2E, -1e9)
            for h in range(heads):
                bias_ref[h, pl.ds(pl.multiple_of(b*rows, rows), rows), :] = piece[h*rows:(h+1)*rows]
            return c
        lax.fori_loop(0, blocks, prep, 0)
        for h in range(heads):
            va_ref[h, :, W:] = jnp.broadcast_to((lane == h).astype(jnp.bfloat16), (n, W))

    x = pair_ref[0].astype(jnp.float32)
    out_ref[0] = pair_ref[0]

    @pl.when(row0 + i < L)
    def _():
        center = jnp.mean(x, axis=-1, keepdims=True)
        xc = x - center
        spread = jnp.mean(xc*xc, axis=-1, keepdims=True)
        normed = (xc*lax.rsqrt(spread+EPS)*gain_ref[...]).astype(jnp.bfloat16)
        def pr(f):
            return jnp.dot(normed, w_ref[f], preferred_element_type=jnp.float32)
        q_ref[...] = (pr(0)*(dh**-0.5*LOG2E)).astype(jnp.bfloat16)
        k_ref[...] = pr(1).astype(jnp.bfloat16)
        v = pr(2).astype(jnp.bfloat16)
        for h in range(heads):
            va_ref[h, :, :W] = jnp.where(lane == h, v, jnp.zeros_like(v))
        g_ref[...] = jax.nn.sigmoid(pr(3))

        def run(nk):
            def qblock(qb, c):
                off = pl.multiple_of(qb*QB, QB)
                qq = q_ref[pl.ds(off, QB), :]
                acc = None
                for h in range(heads):
                    qh = jnp.where(lane == h, qq, jnp.zeros_like(qq))
                    s = lax.dot_general(qh, k_ref[:nk, :], (((1,), (1,)), ((), ())), preferred_element_type=jnp.float32)
                    s = s + bias_ref[h, pl.ds(off, QB), :nk]
                    m = jnp.max(s, axis=-1, keepdims=True)
                    p = jnp.exp2(s-m).astype(jnp.bfloat16)
                    o = jnp.dot(p, va_ref[h, :nk, :], preferred_element_type=jnp.float32)
                    acc = o if acc is None else acc + o
                hd = (acc[:, :W]/acc[:, W:]*g_ref[pl.ds(off, QB), :]).astype(jnp.bfloat16)
                upd = jnp.dot(hd, outw_ref[...], preferred_element_type=jnp.float32)
                base = pair_ref[0, pl.ds(off, QB), :].astype(jnp.float32)
                keep = off + lax.broadcasted_iota(jnp.int32, (QB, 1), 0) < L
                out_ref[0, pl.ds(off, QB), :] = jnp.where(keep, base+upd, base).astype(jnp.bfloat16)
                return c
            lax.fori_loop(0, (L+QB-1)//QB, qblock, 0)
        ng = n//KG
        lo = (n//2)//KG
        for t in range(max(lo, 1), ng+1):
            cond = (L+KG-1)//KG == t
            @pl.when(cond)
            def _(t=t):
                run(t*KG)

def attention(L2, pair, gain, w, plane, outw, *, QB=512, KG=128, heads=4, dh=32):
    rows, n, C = pair.shape
    W = heads*dh
    blocks, hr, _ = plane.shape
    one = pl.Buffered(1)
    full = lambda a: pl.BlockSpec(a.shape, lambda i: (0,)*a.ndim, pipeline_mode=one)
    return pl.pallas_call(
        functools.partial(attn_kernel, QB=QB, KG=KG, n=n, heads=heads, dh=dh),
        grid=(rows,),
        in_specs=[pl.BlockSpec(memory_space=pltpu.SMEM),
                  pl.BlockSpec((1, n, C), lambda i: (i, 0, 0)),
                  full(gain), full(w), full(plane), full(outw)],
        out_specs=pl.BlockSpec((1, n, C), lambda i: (i, 0, 0)),
        out_shape=jax.ShapeDtypeStruct((rows, n, C), jnp.bfloat16),
        scratch_shapes=[pltpu.VMEM((heads, n, n), jnp.float32),
                        pltpu.VMEM((n, W), jnp.bfloat16),
                        pltpu.VMEM((n, W), jnp.bfloat16),
                        pltpu.VMEM((heads, n, 2*W), jnp.bfloat16),
                        pltpu.VMEM((n, W), jnp.float32)],
        compiler_params=pltpu.CompilerParams(vmem_limit_bytes=60*2**20),
    )(L2, pair, gain, w, plane, outw)


def plane_of(pair, gain, bias_w):
    floats = pair.astype(jnp.float32)
    center = jnp.mean(floats, axis=-1, keepdims=True)
    spread = jnp.mean((floats - center) ** 2, axis=-1, keepdims=True)
    normed = ((floats - center) * lax.rsqrt(spread + EPS) * gain).astype(jnp.bfloat16)
    plane = jnp.einsum("abc,ch->hab", normed, bias_w, preferred_element_type=jnp.float32)
    heads, rows, n = plane.shape
    return plane.astype(jnp.bfloat16).reshape(heads * rows, n)


def on_device(pair_map, residue_mask, gain_start, proj_start, bias_start, out_start, gain_end, proj_end, bias_end, out_end):
    both = ("dap", "rep")
    rows = pair_map.shape[0] // lax.axis_size("rep")
    rep = lax.axis_index("rep")
    length = jnp.sum(residue_mask)
    row0 = (lax.axis_index("dap") * lax.axis_size("rep") + rep) * rows
    facts = jnp.stack([length, row0]).astype(jnp.int32)
    proj = lax.all_gather(jnp.stack([proj_start, proj_end]), "rep", axis=3, tiled=True)
    bias = lax.all_gather(jnp.stack([bias_start, bias_end]), "rep", axis=2, tiled=True)

    def module(pair, gain, w, bw, ow):
        plane = lax.all_gather(plane_of(pair, gain, bw), both, axis=0, tiled=False)
        return attention(facts, pair, gain[None, :], w, plane, ow)

    mine = lax.dynamic_slice_in_dim(pair_map, rep * rows, rows, 0)
    mid = module(mine, gain_start, proj[0], bias[0], out_start)
    turned = lax.all_to_all(jnp.transpose(mid, (1, 0, 2)), both, split_axis=0, concat_axis=1, tiled=True)
    done = module(turned, gain_end, proj[1], bias[1], out_end)
    return lax.all_gather(done, "rep", axis=0, tiled=True)


def solution(mesh):
    in_specs = (
        P("dap", None, None), P(), P(), P(None, None, "rep"), P(None, "rep"), P(),
        P(), P(None, None, "rep"), P(None, "rep"), P(),
    )
    return jax.shard_map(on_device, mesh=mesh, in_specs=in_specs, out_specs=P("dap", None, None), check_vma=False)
```

```python
import functools
import math

import jax
import jax.numpy as jnp
from jax import lax
from jax.experimental import pallas as pl
from jax.experimental.pallas import tpu as pltpu
from jax.sharding import PartitionSpec as P

EPS = 1e-5
LOG2E = math.log2(math.e)
HEADS = 4
DH = 32
W = HEADS * DH
VMEM_LIMIT = 60 * 2**20
RING = 4
CORES = 2
MESH = pl.DeviceIdType.MESH


def place():
    dap, rep = lax.axis_index("dap"), lax.axis_index("rep")
    core = lax.rem(dap, CORES)
    z = lax.rem(dap // CORES, RING)
    x = lax.rem(dap // (CORES * RING), RING)
    y = rep * 2 + dap // (CORES * RING * RING)
    return {"c": core, "y": y, "x": x, "z": z}


def block_of(at):
    dap = ((lax.rem(at["y"], 2) * RING + at["x"]) * RING + at["z"]) * CORES + at["c"]
    return dap * 2 + at["y"] // 2


def device_of(at):
    dap = ((lax.rem(at["y"], 2) * RING + at["x"]) * RING + at["z"]) * CORES + at["c"]
    return {"dap": dap, "rep": at["y"] // 2}


def shifted(at, axis, by):
    size = CORES if axis == "c" else RING
    return {**at, axis: lax.rem(at[axis] + by + size, size)}


def greet(partners):
    barrier = pltpu.get_barrier_semaphore()
    for partner in partners:
        pl.semaphore_signal(barrier, inc=1, device_id=device_of(partner), device_id_type=MESH)
    pl.semaphore_wait(barrier, len(partners))


def normalize(floats, gain):
    center = jnp.mean(floats, axis=-1, keepdims=True)
    apart = floats - center
    spread = jnp.mean(apart * apart, axis=-1, keepdims=True)
    return (apart * lax.rsqrt(spread + EPS) * gain).astype(jnp.bfloat16)


ORDERS = ("xyz", "yzx", "zxy")


def gather_parts(n):
    unit = n // 8
    return ((0, 3 * unit), (3 * unit, 3 * unit), (6 * unit, 2 * unit))


def prepare_kernel(*refs, turned, n, rows):
    if turned:
        (src_ref, gain_ref, w_ref, bw_ref, gat_ref, q_out, k_out, v_out, g_out, base_out,
         own32, own, norm_ref, q_ref, k_ref, v_ref, g_ref, core_send, core_recv, send, recv, local_sem,
         inbox, base_ref, float_ref, all_send, all_recv) = refs
    else:
        (src_ref, gain_ref, w_ref, bw_ref, gat_ref, q_out, k_out, v_out, g_out,
         own32, own, norm_ref, q_ref, k_ref, v_ref, g_ref, core_send, core_recv, send, recv, local_sem) = refs
    me = place()
    mine = block_of(me)
    blocks = CORES * RING**3
    others = [shifted(me, axis, by) for axis in "xyz" for by in (1, -1)] + [shifted(me, "c", 1)]

    if turned:
        def partner(k):
            at = {"c": lax.rem(me["c"] + lax.rem(k, CORES), CORES)}
            k = k // CORES
            for axis in "zxy":
                at[axis] = lax.rem(me[axis] + lax.rem(k, RING), RING)
                k = k // RING
            return at

        barrier = pltpu.get_barrier_semaphore()

        def hail(k, carry):
            pl.semaphore_signal(barrier, inc=1, device_id=device_of(partner(k)), device_id_type=MESH)
            return carry

        lax.fori_loop(1, blocks, hail, 0)
        pl.semaphore_wait(barrier, blocks - 1)
        keep = pltpu.make_async_copy(src_ref.at[mine], inbox.at[mine], all_recv.at[mine // 16])
        keep.start()

        def post(k, carry):
            at = partner(k)
            pltpu.make_async_remote_copy(
                src_ref=src_ref.at[block_of(at)], dst_ref=inbox.at[mine], send_sem=all_send,
                recv_sem=all_recv.at[mine // 16], device_id=device_of(at), device_id_type=MESH,
            ).start()
            return carry

        lax.fori_loop(1, blocks, post, 0)
        four = 4 * rows * rows
        to = lax.broadcasted_iota(jnp.int32, (four, four), 0)
        come = lax.broadcasted_iota(jnp.int32, (four, four), 1)
        j, which, i = to // (4 * rows), (to // rows) % 4, to % rows
        turn = (come == (which * rows + i) * rows + j).astype(jnp.bfloat16)
        for group in range(blocks // 16):
            area = inbox.at[pl.ds(group * 16, 16)]
            pltpu.make_async_copy(area, area, all_recv.at[group]).wait()
            for part in range(4):
                first = group * 16 + part * 4
                piece = inbox[first:first + 4].reshape(four, -1)
                result = jnp.dot(turn, piece, preferred_element_type=jnp.float32)
                float_ref[:, first * rows:(first + 4) * rows, :] = result.reshape(rows, 4 * rows, -1)
    else:
        greet(others)

    def plane_row(i, carry):
        floats = float_ref[i] if turned else src_ref[i].astype(jnp.float32)
        normed = normalize(floats, gain_ref[...])
        norm_ref[i] = normed
        if turned:
            base_ref[i] = floats.astype(jnp.bfloat16)
        strip = lax.dot_general(bw_ref[...], normed, (((1,), (1,)), ((), ())), preferred_element_type=jnp.float32)
        for h in range(HEADS):
            own32[pl.ds(h * rows + i, 1), :] = strip[h:h + 1]
        return carry

    lax.fori_loop(0, rows, plane_row, 0)
    own[...] = own32[...].astype(jnp.bfloat16)

    started = []
    local = []
    if turned:
        copy = pltpu.make_async_copy(base_ref, base_out, local_sem.at[4 * rows + 1])
        copy.start()
        local.append(copy)
    copy = pltpu.make_async_copy(own, gat_ref.at[me["c"], me["y"], me["x"], me["z"]], local_sem.at[4 * rows])
    copy.start()
    local.append(copy)

    def project(i):
        normed = norm_ref[i]

        def part(f):
            return jnp.dot(normed, w_ref[f], preferred_element_type=jnp.float32)

        q_ref[i] = (part(0) * (DH**-0.5 * LOG2E)).astype(jnp.bfloat16)
        k_ref[i] = part(1).astype(jnp.bfloat16)
        v_ref[i] = part(2).astype(jnp.bfloat16)
        g_ref[i] = jax.nn.sigmoid(part(3))
        for number, (a, b) in enumerate(((q_ref, q_out), (k_ref, k_out), (v_ref, v_out), (g_ref, g_out))):
            copy = pltpu.make_async_copy(a.at[i], b.at[i], local_sem.at[4 * i + number])
            copy.start()
            local.append(copy)

    def view(part, marks, half=None, split=None):
        first, width = gather_parts(n)[part]
        index = [me["c"]]
        for axis in "yxz":
            mark = marks[axis]
            if axis == split:
                index.append(pl.ds(2 * half, 2))
            elif mark is None:
                index.append(slice(None))
            else:
                index.append(mark)
        lines = pl.ds(16 * half, 16) if half is not None and split is None else slice(None)
        return gat_ref.at[(*index, lines, pl.ds(first, width))]

    def push(src, dst, to, semaphores, number):
        copy = pltpu.make_async_remote_copy(
            src_ref=src, dst_ref=dst, send_sem=semaphores[0].at[number], recv_sem=semaphores[1].at[number],
            device_id=device_of(to), device_id_type=MESH,
        )
        copy.start()
        started.append(copy)
        return copy

    def share(part, number, marks):
        area = view(part, marks)
        return push(area, area, shifted(me, "c", 1), (core_send, core_recv), part * 4 + number)

    pending = {}
    shared = []
    project_next = 0
    for phase in range(3):
        marks = {}
        if phase == 1:
            local[1 if turned else 0].wait()
        for part, order in enumerate(ORDERS):
            axis = order[phase]
            marks[part] = {a: (None if a in order[:phase] else me[a]) for a in "yxz"}
            if phase > 0:
                for copy in pending[part]:
                    copy.wait_recv()
            area = view(part, marks[part])
            source = area
            if phase == 0:
                first, width = gather_parts(n)[part]
                source = own.at[:, pl.ds(first, width)]
            pending[part] = [
                push(source, area, shifted(me, axis, by), (send, recv), ((part * 3 + phase) * 2) * 2 + way)
                for way, by in enumerate((1, -1))
            ]
            if phase == 2:
                shared.append(share(part, 0, marks[part]))
        for _ in range(phase + 1):
            project(project_next)
            project_next += 1
        for part, order in enumerate(ORDERS):
            axis = order[phase]
            split = order[0] if phase > 0 else None
            back = {**marks[part], axis: shifted(me, axis, -1)[axis]}
            ahead = {**marks[part], axis: shifted(me, axis, 1)[axis]}
            later = []
            for way, (by, held) in enumerate(((1, back), (-1, ahead))):
                pending[part][way].wait_recv()
                area = view(part, held, half=way, split=split)
                later.append(push(area, area, shifted(me, axis, by), (send, recv), ((part * 3 + phase) * 2 + 1) * 2 + way))
            if phase == 2:
                shared.append(share(part, 1, back))
                shared.append(share(part, 2, ahead))
            pending[part] = later
        if phase < 2:
            project(project_next)
            project_next += 1
    while project_next < rows:
        project(project_next)
        project_next += 1
    for part, order in enumerate(ORDERS):
        for copy in pending[part]:
            copy.wait_recv()
        axis = order[2]
        far = {**{a: None for a in "yxz"}, axis: shifted(me, axis, 2)[axis]}
        shared.append(share(part, 3, far))
    for copy in shared:
        copy.wait_recv()
    for copy in started:
        copy.wait_send()
    for number, copy in enumerate(local):
        if number != (1 if turned else 0):
            copy.wait()
    if turned:
        area = src_ref.at[pl.ds(0, blocks - 1)]
        pltpu.make_async_copy(area, area, all_send).wait()


def prepare(src, gain, w, bw, *, turned, n, rows, ident):
    c = src.shape[-1]
    shape = (rows, n, W)
    out_shape = [jax.ShapeDtypeStruct((CORES, RING, RING, RING, HEADS * rows, n), jnp.bfloat16)]
    out_shape += [jax.ShapeDtypeStruct(shape, jnp.bfloat16)] * 3 + [jax.ShapeDtypeStruct(shape, jnp.float32)]
    if turned:
        out_shape.append(jax.ShapeDtypeStruct((rows, n, c), jnp.bfloat16))
    scratch = [
        pltpu.VMEM((HEADS * rows, n), jnp.float32),
        pltpu.VMEM((HEADS * rows, n), jnp.bfloat16),
        pltpu.VMEM((rows, n, c), jnp.bfloat16),
        pltpu.VMEM(shape, jnp.bfloat16),
        pltpu.VMEM(shape, jnp.bfloat16),
        pltpu.VMEM(shape, jnp.bfloat16),
        pltpu.VMEM(shape, jnp.float32),
        pltpu.SemaphoreType.DMA((12,)),
        pltpu.SemaphoreType.DMA((12,)),
        pltpu.SemaphoreType.DMA((36,)),
        pltpu.SemaphoreType.DMA((36,)),
        pltpu.SemaphoreType.DMA((4 * rows + 2,)),
    ]
    if turned:
        scratch += [
            pltpu.VMEM(src.shape, jnp.bfloat16),
            pltpu.VMEM((rows, n, c), jnp.bfloat16),
            pltpu.VMEM((rows, n, c), jnp.float32),
            pltpu.SemaphoreType.DMA,
            pltpu.SemaphoreType.DMA((8,)),
        ]
    vmem = pl.BlockSpec(memory_space=pltpu.VMEM)
    hbm = pl.BlockSpec(memory_space=pl.ANY)
    return pl.pallas_call(
        functools.partial(prepare_kernel, turned=turned, n=n, rows=rows),
        out_shape=out_shape,
        in_specs=[hbm if turned else vmem, vmem, vmem, vmem],
        out_specs=[hbm] * len(out_shape),
        scratch_shapes=scratch,
        compiler_params=pltpu.CompilerParams(
            collective_id=ident, has_side_effects=True, vmem_limit_bytes=VMEM_LIMIT
        ),
    )(src, gain, w, bw)


def attend_kernel(facts_ref, base_ref, q_ref, k_ref, v_ref, g_ref, plane_ref, outw_ref, out_ref,
                  bias_ref, va_ref, done_ref, *, n, rows, span, step, blocked):
    pair = pl.program_id(0)
    length = facts_ref[0]
    row0 = facts_ref[1]
    lane = lax.broadcasted_iota(jnp.int32, (1, W), 1) // DH

    @pl.when(pair == 0)
    def _():
        valid = lax.broadcasted_iota(jnp.int32, (1, n), 1) < length

        def unfold(t, carry):
            at = {"z": lax.rem(t, RING), "x": lax.rem(t // RING, RING),
                  "y": lax.rem(t // RING**2, RING), "c": t // RING**3}
            piece = plane_ref[t].astype(jnp.float32)
            piece = jnp.where(valid, piece * LOG2E, -1e9)
            first = pl.multiple_of(block_of(at) * rows, rows)
            for h in range(HEADS):
                bias_ref[h, pl.ds(first, rows), :] = piece[h * rows:(h + 1) * rows]
            return carry

        lax.fori_loop(0, plane_ref.shape[0], unfold, 0)
        for h in range(HEADS):
            va_ref[h, :, W:] = jnp.broadcast_to((lane == h).astype(jnp.bfloat16), (n, W))

    def one_row(i, carry):
        done_ref[i] = base_ref[i].astype(jnp.float32)

        @pl.when(row0 + pair * 2 + i < length)
        def _():
            v = v_ref[i]
            for h in range(HEADS):
                va_ref[h, :, :W] = jnp.where(lane == h, v, jnp.zeros_like(v))

            def run(keys):
                def one_span(number, inner):
                    off = pl.multiple_of(number * span, span)
                    queries = q_ref[i, pl.ds(off, span), :]
                    total = None
                    for h in range(HEADS):
                        own = jnp.where(lane == h, queries, jnp.zeros_like(queries))
                        scores = lax.dot_general(
                            own, k_ref[i, :keys, :], (((1,), (1,)), ((), ())), preferred_element_type=jnp.float32
                        )
                        scores = scores + bias_ref[h, pl.ds(off, span), :keys]
                        highest = jnp.max(scores, axis=-1, keepdims=True)
                        expo = jnp.exp2(scores - highest).astype(jnp.bfloat16)
                        part = jnp.dot(expo, va_ref[h, :keys, :], preferred_element_type=jnp.float32)
                        total = part if total is None else total + part
                    gated = total[:, :W] / total[:, W:] * g_ref[i, pl.ds(off, span), :]
                    update = jnp.dot(gated.astype(jnp.bfloat16), outw_ref[...], preferred_element_type=jnp.float32)
                    base = done_ref[i, pl.ds(off, span), :]
                    keep = off + lax.broadcasted_iota(jnp.int32, (span, 1), 0) < length
                    done_ref[i, pl.ds(off, span), :] = jnp.where(keep, base + update, base)
                    return inner

                lax.fori_loop(0, (length + span - 1) // span, one_span, 0)

            for count in range(n // 2 // step, n // step + 1):
                @pl.when((length + step - 1) // step == count)
                def _(count=count):
                    run(count * step)

        return carry

    lax.fori_loop(0, 2, one_row, 0)
    if blocked:
        both = [done_ref[i].reshape(n // rows, rows, -1) for i in range(2)]
        out_ref[...] = jnp.concatenate(both, axis=1).astype(jnp.bfloat16)
    else:
        out_ref[...] = done_ref[...].astype(jnp.bfloat16)


def attend(facts, base, q, k, v, g, plane, outw, *, blocked, span=512, step=128):
    rows, n, c = base.shape
    plane = plane.reshape(CORES * RING**3, HEADS * rows, n)
    one = pl.Buffered(1)
    full = lambda a: pl.BlockSpec(a.shape, lambda i: (0,) * a.ndim, pipeline_mode=one)
    two = pl.BlockSpec((2, n, c), lambda i: (i, 0, 0))
    if blocked:
        out_shape = (n // rows, rows * rows, c)
        out_spec = pl.BlockSpec((n // rows, 2 * rows, c), lambda i: (0, i, 0))
    else:
        out_shape, out_spec = (rows, n, c), two
    return pl.pallas_call(
        functools.partial(attend_kernel, n=n, rows=rows, span=span, step=step, blocked=blocked),
        grid=(rows // 2,),
        in_specs=[pl.BlockSpec(memory_space=pltpu.SMEM), two, two, two, two, two, full(plane), full(outw)],
        out_specs=out_spec,
        out_shape=jax.ShapeDtypeStruct(out_shape, jnp.bfloat16),
        scratch_shapes=[
            pltpu.VMEM((HEADS, n, n), jnp.float32),
            pltpu.VMEM((HEADS, n, 2 * W), jnp.bfloat16),
            pltpu.VMEM((2, n, c), jnp.float32),
        ],
        compiler_params=pltpu.CompilerParams(vmem_limit_bytes=VMEM_LIMIT),
    )(facts, base, q, k, v, g, plane, outw)


def exchange_kernel(src_ref, out_ref, mid_ref, send, recv, local_sem, *, rows):
    me = place()
    rep = lax.axis_index("rep")
    keep = pltpu.make_async_copy(src_ref, out_ref.at[pl.ds(rep * rows, rows)], local_sem)
    keep.start()
    sides = (shifted(me, "y", 1), shifted(me, "y", -1))
    greet(sides)
    first, second = [], []

    def push(src, dst, to, number):
        copy = pltpu.make_async_remote_copy(
            src_ref=src, dst_ref=dst, send_sem=send.at[number], recv_sem=recv.at[number],
            device_id=device_of(to), device_id_type=MESH,
        )
        copy.start()
        return copy

    order = [way * (rows // 2) + t for t in range(rows // 2) for way in range(2)]
    for row in order:
        first.append(push(src_ref.at[row], mid_ref.at[row], sides[row // (rows // 2)], row))
    for row, copy in zip(order, first):
        copy.wait_recv()
        target = sides[row // (rows // 2)]
        slot = (1 - target["y"] // 2) * rows + row
        second.append(push(mid_ref.at[row], out_ref.at[slot], target, rows + row))
    for copy in second:
        copy.wait_recv()
    for copy in first + second:
        copy.wait_send()
    keep.wait()


def exchange(src, ident):
    rows, n, c = src.shape
    hbm = pl.BlockSpec(memory_space=pl.ANY)
    out, _ = pl.pallas_call(
        functools.partial(exchange_kernel, rows=rows),
        out_shape=[jax.ShapeDtypeStruct((2 * rows, n, c), src.dtype), jax.ShapeDtypeStruct(src.shape, src.dtype)],
        in_specs=[hbm],
        out_specs=[hbm, hbm],
        scratch_shapes=[
            pltpu.SemaphoreType.DMA((2 * rows,)),
            pltpu.SemaphoreType.DMA((2 * rows,)),
            pltpu.SemaphoreType.DMA,
        ],
        compiler_params=pltpu.CompilerParams(collective_id=ident, has_side_effects=True, vmem_limit_bytes=VMEM_LIMIT),
    )(src)
    return out


def on_device(pair_map, residue_mask, gain_start, proj_start, bias_start, out_start, gain_end, proj_end, bias_end, out_end):
    n = pair_map.shape[1]
    rows = pair_map.shape[0] // 2
    rep = lax.axis_index("rep")
    row0 = (lax.axis_index("dap") * 2 + rep) * rows
    facts = jnp.stack([jnp.sum(residue_mask), row0]).astype(jnp.int32)
    proj = lax.all_gather(jnp.stack([proj_start, proj_end]), "rep", axis=3, tiled=True)
    bias = lax.all_gather(jnp.stack([bias_start, bias_end]), "rep", axis=2, tiled=True)
    bias = jnp.pad(jnp.transpose(bias, (0, 2, 1)), ((0, 0), (0, 16 - HEADS), (0, 0)))
    mine = lax.dynamic_slice_in_dim(pair_map, rep * rows, rows, 0)
    plane, q, k, v, g = prepare(
        mine, gain_start[None, :], proj[0], bias[0], turned=False, n=n, rows=rows, ident=0
    )
    mid = attend(facts, mine, q, k, v, g, plane, out_start, blocked=True)
    plane, q, k, v, g, base = prepare(
        mid, gain_end[None, :], proj[1], bias[1], turned=True, n=n, rows=rows, ident=1
    )
    done = attend(facts, base, q, k, v, g, plane, out_end, blocked=False)
    return exchange(done, 2)


def solution(mesh):
    in_specs = (
        P("dap", None, None), P(), P(), P(None, None, "rep"), P(None, "rep"), P(),
        P(), P(None, None, "rep"), P(None, "rep"), P(),
    )
    return jax.shard_map(on_device, mesh=mesh, in_specs=in_specs, out_specs=P("dap", None, None), check_vma=False)
```

```python
import functools
import math

import jax
import jax.numpy as jnp
from jax import lax
from jax.experimental import pallas as pl
from jax.experimental.pallas import tpu as pltpu
from jax.sharding import PartitionSpec as P

EPS = 1e-5
LOG2E = math.log2(math.e)
HEADS = 4
DH = 32
W = HEADS * DH
VMEM_LIMIT = 60 * 2**20
RING = 4
CORES = 2
MESH = pl.DeviceIdType.MESH


def place():
    dap, rep = lax.axis_index("dap"), lax.axis_index("rep")
    core = lax.rem(dap, CORES)
    z = lax.rem(dap // CORES, RING)
    x = lax.rem(dap // (CORES * RING), RING)
    y = rep * 2 + dap // (CORES * RING * RING)
    return {"c": core, "y": y, "x": x, "z": z}


def block_of(at):
    dap = ((lax.rem(at["y"], 2) * RING + at["x"]) * RING + at["z"]) * CORES + at["c"]
    return dap * 2 + at["y"] // 2


def device_of(at):
    dap = ((lax.rem(at["y"], 2) * RING + at["x"]) * RING + at["z"]) * CORES + at["c"]
    return {"dap": dap, "rep": at["y"] // 2}


def shifted(at, axis, by):
    size = CORES if axis == "c" else RING
    return {**at, axis: lax.rem(at[axis] + by + size, size)}


def greet(partners):
    barrier = pltpu.get_barrier_semaphore()
    for partner in partners:
        pl.semaphore_signal(barrier, inc=1, device_id=device_of(partner), device_id_type=MESH)
    pl.semaphore_wait(barrier, len(partners))


def normalize(floats, gain):
    center = jnp.mean(floats, axis=-1, keepdims=True)
    apart = floats - center
    spread = jnp.mean(apart * apart, axis=-1, keepdims=True)
    return (apart * lax.rsqrt(spread + EPS) * gain).astype(jnp.bfloat16)


ORDERS = ("xyz", "yzx", "zxy")


def gather_parts(n):
    unit = n // 8
    return ((0, 3 * unit), (3 * unit, 3 * unit), (6 * unit, 2 * unit))


def prepare_kernel(*refs, turned, n, rows):
    if turned:
        (src_ref, gain_ref, w_ref, bw_ref, gat_ref, q_out, k_out, v_out, g_out, base_out,
         own32, own, norm_ref, q_ref, k_ref, v_ref, g_ref, core_send, core_recv, send, recv, local_sem,
         base_ref, float_ref) = refs
    else:
        (src_ref, gain_ref, w_ref, bw_ref, gat_ref, q_out, k_out, v_out, g_out,
         own32, own, norm_ref, q_ref, k_ref, v_ref, g_ref, core_send, core_recv, send, recv, local_sem) = refs
    me = place()
    others = [shifted(me, axis, by) for axis in "xyz" for by in (1, -1)] + [shifted(me, "c", 1)]

    greet(others)
    if turned:
        four = 4 * rows * rows
        to = lax.broadcasted_iota(jnp.int32, (four, four), 0)
        come = lax.broadcasted_iota(jnp.int32, (four, four), 1)
        j, which, i = to // (4 * rows), (to // rows) % 4, to % rows
        turn = (come == ((i // 2 * 4 + which) * 2 + i % 2) * rows + j).astype(jnp.bfloat16)
        for low in range(2):
            for xz in range(RING * RING):
                piece = src_ref[:, xz, 4 * low:4 * low + 4].reshape(four, -1)
                result = jnp.dot(turn, piece, preferred_element_type=jnp.float32)
                first = (low * RING * RING + xz) * 4
                float_ref[:, first * rows:(first + 4) * rows, :] = result.reshape(rows, 4 * rows, -1)

    def plane_row(i, carry):
        floats = float_ref[i] if turned else src_ref[i].astype(jnp.float32)
        normed = normalize(floats, gain_ref[...])
        norm_ref[i] = normed
        if turned:
            base_ref[i] = floats.astype(jnp.bfloat16)
        strip = lax.dot_general(bw_ref[...], normed, (((1,), (1,)), ((), ())), preferred_element_type=jnp.float32)
        for h in range(HEADS):
            own32[pl.ds(h * rows + i, 1), :] = strip[h:h + 1]
        return carry

    lax.fori_loop(0, rows, plane_row, 0)
    own[...] = own32[...].astype(jnp.bfloat16)

    started = []
    local = []
    if turned:
        copy = pltpu.make_async_copy(base_ref, base_out, local_sem.at[4 * rows + 1])
        copy.start()
        local.append(copy)
    copy = pltpu.make_async_copy(own, gat_ref.at[me["c"], me["y"], me["x"], me["z"]], local_sem.at[4 * rows])
    copy.start()
    local.append(copy)

    def project(i):
        normed = norm_ref[i]

        def part(f):
            return jnp.dot(normed, w_ref[f], preferred_element_type=jnp.float32)

        q_ref[i] = (part(0) * (DH**-0.5 * LOG2E)).astype(jnp.bfloat16)
        k_ref[i] = part(1).astype(jnp.bfloat16)
        v_ref[i] = part(2).astype(jnp.bfloat16)
        g_ref[i] = jax.nn.sigmoid(part(3))
        for number, (a, b) in enumerate(((q_ref, q_out), (k_ref, k_out), (v_ref, v_out), (g_ref, g_out))):
            copy = pltpu.make_async_copy(a.at[i], b.at[i], local_sem.at[4 * i + number])
            copy.start()
            local.append(copy)

    def view(part, marks, half=None, split=None):
        first, width = gather_parts(n)[part]
        index = [me["c"]]
        for axis in "yxz":
            mark = marks[axis]
            if axis == split:
                index.append(pl.ds(2 * half, 2))
            elif mark is None:
                index.append(slice(None))
            else:
                index.append(mark)
        lines = pl.ds(16 * half, 16) if half is not None and split is None else slice(None)
        return gat_ref.at[(*index, lines, pl.ds(first, width))]

    def push(src, dst, to, semaphores, number):
        copy = pltpu.make_async_remote_copy(
            src_ref=src, dst_ref=dst, send_sem=semaphores[0].at[number], recv_sem=semaphores[1].at[number],
            device_id=device_of(to), device_id_type=MESH,
        )
        copy.start()
        started.append(copy)
        return copy

    def share(part, number, marks):
        area = view(part, marks)
        return push(area, area, shifted(me, "c", 1), (core_send, core_recv), part * 4 + number)

    pending = {}
    shared = []
    project_next = 0
    for phase in range(3):
        marks = {}
        if phase == 1:
            local[1 if turned else 0].wait()
        for part, order in enumerate(ORDERS):
            axis = order[phase]
            marks[part] = {a: (None if a in order[:phase] else me[a]) for a in "yxz"}
            if phase > 0:
                for copy in pending[part]:
                    copy.wait_recv()
            area = view(part, marks[part])
            source = area
            if phase == 0:
                first, width = gather_parts(n)[part]
                source = own.at[:, pl.ds(first, width)]
            pending[part] = [
                push(source, area, shifted(me, axis, by), (send, recv), ((part * 3 + phase) * 2) * 2 + way)
                for way, by in enumerate((1, -1))
            ]
            if phase == 2:
                shared.append(share(part, 0, marks[part]))
        for _ in range(phase + 1):
            project(project_next)
            project_next += 1
        for part, order in enumerate(ORDERS):
            axis = order[phase]
            split = order[0] if phase > 0 else None
            back = {**marks[part], axis: shifted(me, axis, -1)[axis]}
            ahead = {**marks[part], axis: shifted(me, axis, 1)[axis]}
            later = []
            for way, (by, held) in enumerate(((1, back), (-1, ahead))):
                pending[part][way].wait_recv()
                area = view(part, held, half=way, split=split)
                later.append(push(area, area, shifted(me, axis, by), (send, recv), ((part * 3 + phase) * 2 + 1) * 2 + way))
            if phase == 2:
                shared.append(share(part, 1, back))
                shared.append(share(part, 2, ahead))
            pending[part] = later
        if phase < 2:
            project(project_next)
            project_next += 1
    while project_next < rows:
        project(project_next)
        project_next += 1
    for part, order in enumerate(ORDERS):
        for copy in pending[part]:
            copy.wait_recv()
        axis = order[2]
        far = {**{a: None for a in "yxz"}, axis: shifted(me, axis, 2)[axis]}
        shared.append(share(part, 3, far))
    for copy in shared:
        copy.wait_recv()
    for copy in started:
        copy.wait_send()
    for number, copy in enumerate(local):
        if number != (1 if turned else 0):
            copy.wait()


def prepare(src, gain, w, bw, *, turned, n, rows, ident):
    c = src.shape[-1]
    shape = (rows, n, W)
    out_shape = [jax.ShapeDtypeStruct((CORES, RING, RING, RING, HEADS * rows, n), jnp.bfloat16)]
    out_shape += [jax.ShapeDtypeStruct(shape, jnp.bfloat16)] * 3 + [jax.ShapeDtypeStruct(shape, jnp.float32)]
    if turned:
        out_shape.append(jax.ShapeDtypeStruct((rows, n, c), jnp.bfloat16))
    scratch = [
        pltpu.VMEM((HEADS * rows, n), jnp.float32),
        pltpu.VMEM((HEADS * rows, n), jnp.bfloat16),
        pltpu.VMEM((rows, n, c), jnp.bfloat16),
        pltpu.VMEM(shape, jnp.bfloat16),
        pltpu.VMEM(shape, jnp.bfloat16),
        pltpu.VMEM(shape, jnp.bfloat16),
        pltpu.VMEM(shape, jnp.float32),
        pltpu.SemaphoreType.DMA((12,)),
        pltpu.SemaphoreType.DMA((12,)),
        pltpu.SemaphoreType.DMA((36,)),
        pltpu.SemaphoreType.DMA((36,)),
        pltpu.SemaphoreType.DMA((4 * rows + 2,)),
    ]
    if turned:
        scratch += [
            pltpu.VMEM((rows, n, c), jnp.bfloat16),
            pltpu.VMEM((rows, n, c), jnp.float32),
        ]
    vmem = pl.BlockSpec(memory_space=pltpu.VMEM)
    hbm = pl.BlockSpec(memory_space=pl.ANY)
    return pl.pallas_call(
        functools.partial(prepare_kernel, turned=turned, n=n, rows=rows),
        out_shape=out_shape,
        in_specs=[vmem, vmem, vmem, vmem],
        out_specs=[hbm] * len(out_shape),
        scratch_shapes=scratch,
        compiler_params=pltpu.CompilerParams(
            collective_id=ident, has_side_effects=True, vmem_limit_bytes=VMEM_LIMIT
        ),
    )(src, gain, w, bw)


def attend_kernel(facts_ref, base_ref, q_ref, k_ref, v_ref, g_ref, plane_ref, outw_ref, out_ref, *scratch,
                  n, rows, keys, turning):
    (bias_ref, va_ref, done_ref, score_ref, expo_ref, total_ref, stage_ref,
     send, recv, local_sem) = scratch[:10]
    pair = pl.program_id(0)
    steps = rows // 2
    length = facts_ref[0]
    row0 = facts_ref[1]
    lane = lax.broadcasted_iota(jnp.int32, (1, W), 1) // DH
    span = keys // 2
    me = place()
    rep = lax.axis_index("rep")
    peer = shifted(me, "y", 2)
    column = [{**me, "y": lax.rem(me["y"] + k // CORES, RING), "c": lax.rem(me["c"] + k % CORES, CORES)}
              for k in range(CORES * RING)]
    level = [{**me, "x": lax.rem(me["x"] + k // RING, RING), "z": lax.rem(me["z"] + k % RING, RING)}
             for k in range(RING * RING)]
    partners = column[1:] + level[1:] if turning else [peer]

    @pl.when(pair == 0)
    def _():
        barrier = pltpu.get_barrier_semaphore()
        for partner in partners:
            pl.semaphore_signal(barrier, inc=1, device_id=device_of(partner), device_id_type=MESH)
        valid = lax.broadcasted_iota(jnp.int32, (1, n), 1) < length

        def unfold(t, carry):
            at = {"z": lax.rem(t, RING), "x": lax.rem(t // RING, RING),
                  "y": lax.rem(t // RING**2, RING), "c": t // RING**3}
            piece = plane_ref[t].astype(jnp.float32)
            piece = jnp.where(valid, piece * LOG2E, -1e9)
            first = pl.multiple_of(block_of(at) * rows, rows)
            for h in range(HEADS):
                bias_ref[h, pl.ds(first, rows), :] = piece[h * rows:(h + 1) * rows]
            return carry

        lax.fori_loop(0, plane_ref.shape[0], unfold, 0)
        for h in range(HEADS):
            va_ref[h, :, W:] = jnp.broadcast_to((lane == h).astype(jnp.bfloat16), (n, W))
        pl.semaphore_wait(barrier, len(partners))

    units = [(off, h) for off in (0, span) for h in range(HEADS)]
    tiles = [(first, min(256, keys - first)) for first in range(0, keys, 256)]
    grains = span // 16
    cuts = [16 * (grains * t // len(tiles)) for t in range(len(tiles) + 1)]

    def row_copies(row):
        slot = rep * rows + row
        remote = pltpu.make_async_remote_copy(
            src_ref=stage_ref.at[row], dst_ref=out_ref.at[slot], send_sem=send.at[row], recv_sem=recv.at[row],
            device_id=device_of(peer), device_id_type=MESH,
        )
        return remote, pltpu.make_async_copy(stage_ref.at[row], out_ref.at[slot], local_sem.at[row])

    def one_row(i, carry):
        limit = jnp.where(row0 + pair * 2 + i < length, length, 0)
        v = v_ref[i]
        for h in range(HEADS):
            va_ref[h, :, :W] = jnp.where(lane == h, v, jnp.zeros_like(v))

        def score(unit, t):
            off, h = units[unit]
            first, width = tiles[t]
            queries = q_ref[i, off:off + span, :]
            own = jnp.where(lane == h, queries, jnp.zeros_like(queries))
            score_ref[unit % 2, :, first:first + width] = lax.dot_general(
                own, k_ref[i, first:first + width, :], (((1,), (1,)), ((), ())), preferred_element_type=jnp.float32
            )

        def soften(unit, t):
            off, h = units[unit]
            for lo in range(cuts[t], cuts[t + 1], GRAIN):
                hi = min(lo + GRAIN, cuts[t + 1])
                scores = score_ref[unit % 2, lo:hi, :] + bias_ref[h, off + lo:off + hi, :keys]
                highest = jnp.max(scores, axis=-1, keepdims=True)
                expo_ref[unit % 2, lo:hi, :] = jnp.exp2(scores - highest).astype(jnp.bfloat16)

        def combine(unit, t):
            h = units[unit][1]
            first, width = tiles[t]
            part = jnp.dot(
                expo_ref[unit % 2, :, first:first + width], va_ref[h, first:first + width, :],
                preferred_element_type=jnp.float32,
            )
            if h == 0 and t == 0:
                total_ref[...] = part
            else:
                total_ref[...] += part

        def finish(off):
            gated = total_ref[:, :W] / total_ref[:, W:] * g_ref[i, off:off + span, :]
            update = jnp.dot(gated.astype(jnp.bfloat16), outw_ref[...], preferred_element_type=jnp.float32)
            base = base_ref[i, off:off + span, :].astype(jnp.float32)
            keep = off + lax.broadcasted_iota(jnp.int32, (span, 1), 0) < limit
            result = jnp.where(keep, base + update, base)
            if turning:
                done_ref[i, off:off + span, :] = result
            else:
                stage_ref[pair * 2 + i, off:off + span, :] = result.astype(jnp.bfloat16)

        for stage in range(len(units) + 2):
            for t in range(len(tiles)):
                if stage < len(units):
                    score(stage, t)
                if stage >= 2:
                    combine(stage - 2, t)
                if 1 <= stage <= len(units):
                    soften(stage - 1, t)
            if stage >= 2 and units[stage - 2][1] == HEADS - 1:
                finish(units[stage - 2][0])
        if keys < n:
            if turning:
                done_ref[i, keys:, :] = base_ref[i, keys:, :].astype(jnp.float32)
            else:
                stage_ref[pair * 2 + i, keys:, :] = base_ref[i, keys:, :]
        if not turning:
            for copy in row_copies(pair * 2 + i):
                copy.start()
        return carry

    lax.fori_loop(0, 2, one_row, 0)
    if not turning:
        @pl.when(pair == steps - 1)
        def _():
            for row in range(rows):
                remote, keep = row_copies(row)
                remote.wait()
                keep.wait()
        return

    mail_ref, send_far, recv_far, far_sem = scratch[10:]
    mine_yc = lax.rem(me["y"], 2) * 4 + me["c"] * 2 + me["y"] // 2
    mine_xz = me["x"] * RING + me["z"]

    def first_copy(p, k):
        at = column[k]
        source = stage_ref.at[p, lax.rem(at["y"], 2), :, at["c"] * 2 + at["y"] // 2]
        goal = mail_ref.at[p, mine_yc]
        if k == 0:
            return pltpu.make_async_copy(source, goal, local_sem.at[p])
        number = p * CORES * RING + k
        return pltpu.make_async_remote_copy(
            src_ref=source, dst_ref=goal, send_sem=send.at[number], recv_sem=recv.at[number],
            device_id=device_of(at), device_id_type=MESH,
        )

    def second_copy(p, k):
        at = level[k]
        source = mail_ref.at[p, :, at["x"] * RING + at["z"]]
        goal = out_ref.at[p, mine_xz]
        if k == 0:
            return pltpu.make_async_copy(source, goal, far_sem.at[p])
        number = p * RING * RING + k
        return pltpu.make_async_remote_copy(
            src_ref=source, dst_ref=goal, send_sem=send_far.at[number], recv_sem=recv_far.at[number],
            device_id=device_of(at), device_id_type=MESH,
        )

    def pass_on(p):
        first_copy(p, 0).wait()
        for k in range(1, CORES * RING):
            first_copy(p, k).wait_recv()
        for k in range(RING * RING):
            second_copy(p, k).start()

    both = [done_ref[i].reshape(n // rows, rows, -1) for i in range(2)]
    stage_ref[pair] = jnp.concatenate(both, axis=1).astype(jnp.bfloat16).reshape(stage_ref.shape[1:])
    for k in range(CORES * RING):
        first_copy(pair, k).start()

    @pl.when(pair > 0)
    def _():
        pass_on(pair - 1)

    @pl.when(pair == steps - 1)
    def _():
        pass_on(steps - 1)
        for p in range(steps):
            for k in range(1, CORES * RING):
                first_copy(p, k).wait_send()
            second_copy(p, 0).wait()
            for k in range(1, RING * RING):
                second_copy(p, k).wait_send()
                second_copy(p, k).wait_recv()


GRAIN = 32


def attend(facts, base, q, k, v, g, plane, outw, *, turning, keys, ident):
    rows, n, c = base.shape
    plane = plane.reshape(CORES * RING**3, HEADS * rows, n)
    steps = rows // 2
    one = pl.Buffered(1)
    full = lambda a: pl.BlockSpec(a.shape, lambda i: (0,) * a.ndim, pipeline_mode=one)
    two = pl.BlockSpec((2, n, c), lambda i: (i, 0, 0))
    yc, xz = CORES * RING, RING * RING
    span = keys // 2
    scratch = [
        pltpu.VMEM((HEADS, n, n), jnp.float32),
        pltpu.VMEM((HEADS, n, 2 * W), jnp.bfloat16),
        pltpu.VMEM((2, n, c), jnp.float32),
        pltpu.VMEM((2, span, keys), jnp.float32),
        pltpu.VMEM((2, span, keys), jnp.bfloat16),
        pltpu.VMEM((span, 2 * W), jnp.float32),
    ]
    if turning:
        out_shape = (steps, xz, yc, 2 * rows, c)
        scratch += [
            pltpu.VMEM((steps, 2, xz, yc // 2, 2 * rows, c), jnp.bfloat16),
            pltpu.SemaphoreType.DMA((steps * yc,)),
            pltpu.SemaphoreType.DMA((steps * yc,)),
            pltpu.SemaphoreType.DMA((steps,)),
            pltpu.VMEM((steps, yc, xz, 2 * rows, c), jnp.bfloat16),
            pltpu.SemaphoreType.DMA((steps * xz,)),
            pltpu.SemaphoreType.DMA((steps * xz,)),
            pltpu.SemaphoreType.DMA((steps,)),
        ]
    else:
        out_shape = (2 * rows, n, c)
        scratch += [
            pltpu.VMEM((rows, n, c), jnp.bfloat16),
            pltpu.SemaphoreType.DMA((rows,)),
            pltpu.SemaphoreType.DMA((rows,)),
            pltpu.SemaphoreType.DMA((rows,)),
        ]
    return pl.pallas_call(
        functools.partial(attend_kernel, n=n, rows=rows, keys=keys, turning=turning),
        grid=(steps,),
        in_specs=[pl.BlockSpec(memory_space=pltpu.SMEM), two, two, two, two, two, full(plane), full(outw)],
        out_specs=pl.BlockSpec(memory_space=pl.ANY),
        out_shape=jax.ShapeDtypeStruct(out_shape, jnp.bfloat16),
        scratch_shapes=scratch,
        compiler_params=pltpu.CompilerParams(
            collective_id=ident, has_side_effects=True, vmem_limit_bytes=VMEM_LIMIT
        ),
    )(facts, base, q, k, v, g, plane, outw)


def attend_switch(length, ident, turning, *operands):
    n = operands[1].shape[1]
    step = n // 8
    counts = range(5, 9)
    branches = [
        functools.partial(attend, turning=turning, keys=count * step, ident=ident + number)
        for number, count in enumerate(counts)
    ]
    return lax.switch((length + step - 1) // step - 5, branches, *operands)


def on_device(pair_map, residue_mask, gain_start, proj_start, bias_start, out_start, gain_end, proj_end, bias_end, out_end):
    n = pair_map.shape[1]
    rows = pair_map.shape[0] // 2
    rep = lax.axis_index("rep")
    row0 = (lax.axis_index("dap") * 2 + rep) * rows
    facts = jnp.stack([jnp.sum(residue_mask), row0]).astype(jnp.int32)
    proj = lax.all_gather(jnp.stack([proj_start, proj_end]), "rep", axis=3, tiled=True)
    bias = lax.all_gather(jnp.stack([bias_start, bias_end]), "rep", axis=2, tiled=True)
    bias = jnp.pad(jnp.transpose(bias, (0, 2, 1)), ((0, 0), (0, 16 - HEADS), (0, 0)))
    mine = lax.dynamic_slice_in_dim(pair_map, rep * rows, rows, 0)
    plane, q, k, v, g = prepare(
        mine, gain_start[None, :], proj[0], bias[0], turned=False, n=n, rows=rows, ident=0
    )
    mid = attend_switch(facts[0], 10, True, facts, mine, q, k, v, g, plane, out_start)
    plane, q, k, v, g, base = prepare(
        mid, gain_end[None, :], proj[1], bias[1], turned=True, n=n, rows=rows, ident=1
    )
    return attend_switch(facts[0], 20, False, facts, base, q, k, v, g, plane, out_end)


def solution(mesh):
    in_specs = (
        P("dap", None, None), P(), P(), P(None, None, "rep"), P(None, "rep"), P(),
        P(), P(None, None, "rep"), P(None, "rep"), P(),
    )
    return jax.shard_map(on_device, mesh=mesh, in_specs=in_specs, out_specs=P("dap", None, None), check_vma=False)
```

```python
import functools
import math

import jax
import jax.numpy as jnp
from jax import lax
from jax.experimental import pallas as pl
from jax.experimental.pallas import tpu as pltpu
from jax.sharding import PartitionSpec as P

EPS = 1e-5
LOG2E = math.log2(math.e)
HEADS = 4
DH = 32
W = HEADS * DH
VMEM_LIMIT = 60 * 2**20
RING = 4
CORES = 2
MESH = pl.DeviceIdType.MESH


def place():
    dap, rep = lax.axis_index("dap"), lax.axis_index("rep")
    core = lax.rem(dap, CORES)
    z = lax.rem(dap // CORES, RING)
    x = lax.rem(dap // (CORES * RING), RING)
    y = rep * 2 + dap // (CORES * RING * RING)
    return {"c": core, "y": y, "x": x, "z": z}


def block_of(at):
    dap = ((lax.rem(at["y"], 2) * RING + at["x"]) * RING + at["z"]) * CORES + at["c"]
    return dap * 2 + at["y"] // 2


def device_of(at):
    dap = ((lax.rem(at["y"], 2) * RING + at["x"]) * RING + at["z"]) * CORES + at["c"]
    return {"dap": dap, "rep": at["y"] // 2}


def shifted(at, axis, by):
    size = CORES if axis == "c" else RING
    return {**at, axis: lax.rem(at[axis] + by + size, size)}


def normalize(floats, gain):
    center = jnp.mean(floats, axis=-1, keepdims=True)
    apart = floats - center
    spread = jnp.mean(apart * apart, axis=-1, keepdims=True)
    return (apart * lax.rsqrt(spread + EPS) * gain).astype(jnp.bfloat16)


ORDERS = ("xyz", "yzx", "zxy")
GRAIN = 32


def gather_parts(n):
    unit = n // 8
    return ((0, 3 * unit), (3 * unit, 3 * unit), (6 * unit, 2 * unit))


def module_kernel(*refs, first_module, n, rows):
    if first_module:
        (map_ref, mask_ref, gain_ref, half_ref, strip_ref, outw_ref, out_ref, w_out, bw_out) = refs[:9]
        (gat_ref, bias_ref, norm_ref, q_ref, k_ref, v_ref, g_ref, va_ref, score_ref, expo_ref, total_ref, base_ref,
         own32, stage_ref, core_send, core_recv, send, recv, local_sem, row_send, row_recv, row_local,
         done_ref, mail_ref, far_send, far_recv, far_local, w_ref, strip_in, w_send, w_recv) = refs[9:]
    else:
        (map_ref, mask_ref, gain_ref, w_ref, bw_ref, outw_ref, out_ref) = refs[:7]
        (gat_ref, bias_ref, norm_ref, q_ref, k_ref, v_ref, g_ref, va_ref, score_ref, expo_ref, total_ref, base_ref,
         own32, stage_ref, core_send, core_recv, send, recv, local_sem, row_send, row_recv, row_local) = refs[7:]
    me = place()
    rep = lax.axis_index("rep")
    peer = shifted(me, "y", 2)
    row0 = block_of(me) * rows
    steps = rows // 2
    span = n // 2
    column = [{**me, "y": lax.rem(me["y"] + k // CORES, RING), "c": lax.rem(me["c"] + k % CORES, CORES)}
              for k in range(CORES * RING)]
    level = [{**me, "x": lax.rem(me["x"] + k // RING, RING), "z": lax.rem(me["z"] + k % RING, RING)}
             for k in range(RING * RING)]
    lane = lax.broadcasted_iota(jnp.int32, (1, W), 1) // DH
    mask = mask_ref[...].astype(jnp.float32)
    length = jnp.sum(mask, axis=1, keepdims=True)
    valid = mask > 0.5

    if first_module:
        partners = column[1:] + level[1:]
    else:
        partners = [shifted(me, axis, by) for axis in "xyz" for by in (1, -1)] + [shifted(me, "c", 1), peer]
    barrier = pltpu.get_barrier_semaphore()
    for partner in partners:
        pl.semaphore_signal(barrier, inc=1, device_id=device_of(partner), device_id_type=MESH)

    started = []

    def push(src, dst, to, semaphores, number):
        copy = pltpu.make_async_remote_copy(
            src_ref=src, dst_ref=dst, send_sem=semaphores[0].at[number], recv_sem=semaphores[1].at[number],
            device_id=device_of(to), device_id_type=MESH,
        )
        copy.start()
        started.append(copy)
        return copy

    if first_module:
        fetch = pltpu.make_async_copy(map_ref.at[pl.ds(rep * rows, rows)], base_ref, local_sem.at[0])
        fetch.start()
        place_w = w_ref.at[:, :, pl.ds(rep * (W // 2), W // 2), :]
        keep_w = pltpu.make_async_copy(half_ref, place_w, local_sem.at[1])
        keep_w.start()
        pl.semaphore_wait(barrier, len(partners))
        strip_copy = push(strip_ref, strip_in, peer, (w_send, w_recv), 0)
        w_copy = push(half_ref, place_w, peer, (w_send, w_recv), 1)
        fetch.wait()
    else:
        four = 4 * rows * rows
        to = lax.broadcasted_iota(jnp.int32, (four, four), 0)
        come = lax.broadcasted_iota(jnp.int32, (four, four), 1)
        j, which, i = to // (4 * rows), (to // rows) % 4, to % rows
        turn = (come == ((i // 2 * 4 + which) * 2 + i % 2) * rows + j).astype(jnp.bfloat16)
        for low in range(2):
            for xz in range(RING * RING):
                piece = map_ref[:, xz, 4 * low:4 * low + 4].reshape(four, -1)
                result = jnp.dot(turn, piece, preferred_element_type=jnp.float32)
                first = (low * RING * RING + xz) * 4 * rows
                base_ref[:, first:first + 4 * rows, :] = result.reshape(rows, 4 * rows, -1).astype(jnp.bfloat16)

    def norm_row(i, carry):
        norm_ref[i] = normalize(base_ref[i].astype(jnp.float32), gain_ref[...])
        return carry

    lax.fori_loop(0, rows, norm_row, 0)
    if first_module:
        strip_copy.wait_recv()
        weights = strip_ref[0] + strip_in[0]
        later = strip_ref[1] + strip_in[1]
        bw_out[...] = later
    else:
        weights = bw_ref[...]

    def plane_row(i, carry):
        strip = lax.dot_general(weights, norm_ref[i], (((1,), (1,)), ((), ())), preferred_element_type=jnp.float32)
        for h in range(HEADS):
            own32[pl.ds(h * rows + i, 1), :] = strip[h:h + 1]
        return carry

    lax.fori_loop(0, rows, plane_row, 0)
    gat_ref[me["c"], me["y"], me["x"], me["z"]] = own32[...].astype(jnp.bfloat16)
    if not first_module:
        pl.semaphore_wait(barrier, len(partners))

    def project(i):
        normed = norm_ref[i]

        def part(f):
            w = w_ref[0, f] if first_module else w_ref[f]
            return lax.dot_general(normed, w, (((1,), (1,)), ((), ())), preferred_element_type=jnp.float32)

        q_ref[i] = (part(0) * (DH**-0.5 * LOG2E)).astype(jnp.bfloat16)
        k_ref[i] = part(1).astype(jnp.bfloat16)
        v_ref[i] = part(2).astype(jnp.bfloat16)
        g_ref[i] = jax.nn.sigmoid(part(3))

    def view(part, marks, half=None, split=None):
        first, width = gather_parts(n)[part]
        index = [me["c"]]
        for axis in "yxz":
            mark = marks[axis]
            if axis == split:
                index.append(pl.ds(2 * half, 2))
            elif mark is None:
                index.append(slice(None))
            else:
                index.append(mark)
        lines = pl.ds(16 * half, 16) if half is not None and split is None else slice(None)
        return gat_ref.at[(*index, lines, pl.ds(first, width))]

    def share(part, number, marks):
        area = view(part, marks)
        return push(area, area, shifted(me, "c", 1), (core_send, core_recv), part * 4 + number)

    def unfold(part, core, marks):
        first, width = gather_parts(n)[part]
        free = [axis for axis in "yxz" if marks[axis] is None]

        def one(t, carry):
            at = {**marks, free[0]: t // RING, free[1]: lax.rem(t, RING), "c": core}
            piece = gat_ref[core, at["y"], at["x"], at["z"], :, first:first + width].astype(jnp.float32)
            piece = jnp.where(valid[:, first:first + width], piece * LOG2E, -1e9)
            line = pl.multiple_of(block_of(at) * rows, rows)
            for h in range(HEADS):
                bias_ref[h, pl.ds(line, rows), first:first + width] = piece[h * rows:(h + 1) * rows]
            return carry

        lax.fori_loop(0, RING * RING, one, 0)

    sibling = shifted(me, "c", 1)["c"]
    pending = {}
    shared = {}
    sets = {}
    for phase in range(3):
        marks = {}
        for part, order in enumerate(ORDERS):
            axis = order[phase]
            marks[part] = {a: (None if a in order[:phase] else me[a]) for a in "yxz"}
            if phase > 0:
                for copy in pending[part]:
                    copy.wait_recv()
            area = view(part, marks[part])
            pending[part] = [
                push(area, area, shifted(me, axis, by), (send, recv), ((part * 3 + phase) * 2) * 2 + way)
                for way, by in enumerate((1, -1))
            ]
            if phase == 2:
                shared[part, 0] = share(part, 0, marks[part])
                sets[part, 0] = marks[part]
        if phase == 2:
            if first_module:
                keep_w.wait()
                w_copy.wait_recv()
            for i in range(4):
                project(i)
            for part in range(3):
                unfold(part, me["c"], sets[part, 0])
        for part, order in enumerate(ORDERS):
            axis = order[phase]
            split = order[0] if phase > 0 else None
            back = {**marks[part], axis: shifted(me, axis, -1)[axis]}
            ahead = {**marks[part], axis: shifted(me, axis, 1)[axis]}
            later_copies = []
            for way, (by, held) in enumerate(((1, back), (-1, ahead))):
                pending[part][way].wait_recv()
                area = view(part, held, half=way, split=split)
                later_copies.append(
                    push(area, area, shifted(me, axis, by), (send, recv), ((part * 3 + phase) * 2 + 1) * 2 + way)
                )
            if phase == 2:
                for number, held in ((1, back), (2, ahead)):
                    shared[part, number] = share(part, number, held)
                    sets[part, number] = held
            pending[part] = later_copies
    for i in range(4, rows):
        project(i)
    for part in range(3):
        for number in (1, 2):
            unfold(part, me["c"], sets[part, number])
        shared[part, 0].wait_recv()
        unfold(part, sibling, sets[part, 0])
    for h in range(HEADS):
        va_ref[h, :, W:] = jnp.broadcast_to((lane == h).astype(jnp.bfloat16), (n, W))
    for part, order in enumerate(ORDERS):
        for copy in pending[part]:
            copy.wait_recv()
        axis = order[2]
        sets[part, 3] = {**{a: None for a in "yxz"}, axis: shifted(me, axis, 2)[axis]}
        shared[part, 3] = share(part, 3, sets[part, 3])
    for part in range(3):
        unfold(part, me["c"], sets[part, 3])
        for number in (1, 2):
            shared[part, number].wait_recv()
            unfold(part, sibling, sets[part, number])
    for part in range(3):
        shared[part, 3].wait_recv()
        unfold(part, sibling, sets[part, 3])
    for copy in started:
        copy.wait_send()
    if first_module:
        give_w = pltpu.make_async_copy(w_ref.at[1], w_out, local_sem.at[0])
        give_w.start()

    units = [(off, h) for off in (0, span) for h in range(HEADS)]
    tiles = [(first, min(256, n - first)) for first in range(0, n, 256)]
    grains = span // 16
    cuts = [16 * (grains * t // len(tiles)) for t in range(len(tiles) + 1)]

    def row_copies(row):
        slot = rep * rows + row
        remote = pltpu.make_async_remote_copy(
            src_ref=stage_ref.at[row], dst_ref=out_ref.at[slot], send_sem=row_send.at[row], recv_sem=row_recv.at[row],
            device_id=device_of(peer), device_id_type=MESH,
        )
        return remote, pltpu.make_async_copy(stage_ref.at[row], out_ref.at[slot], row_local.at[row])

    def one_row(row, i):
        inside = (row0 + row).astype(jnp.float32) < length
        v = v_ref[row]
        for h in range(HEADS):
            va_ref[h, :, :W] = jnp.where(lane == h, v, jnp.zeros_like(v))

        def score(unit, t):
            off, h = units[unit]
            first, width = tiles[t]
            queries = q_ref[row, off:off + span, :]
            own = jnp.where(lane == h, queries, jnp.zeros_like(queries))
            score_ref[unit % 2, :, first:first + width] = lax.dot_general(
                own, k_ref[row, first:first + width, :], (((1,), (1,)), ((), ())), preferred_element_type=jnp.float32
            )

        def soften(unit, t):
            off, h = units[unit]
            for lo in range(cuts[t], cuts[t + 1], GRAIN):
                hi = min(lo + GRAIN, cuts[t + 1])
                scores = score_ref[unit % 2, lo:hi, :] + bias_ref[h, off + lo:off + hi, :]
                highest = jnp.max(scores, axis=-1, keepdims=True)
                expo_ref[unit % 2, lo:hi, :] = jnp.exp2(scores - highest).astype(jnp.bfloat16)

        def combine(unit, t):
            h = units[unit][1]
            first, width = tiles[t]
            part = jnp.dot(
                expo_ref[unit % 2, :, first:first + width], va_ref[h, first:first + width, :],
                preferred_element_type=jnp.float32,
            )
            if h == 0 and t == 0:
                total_ref[...] = part
            else:
                total_ref[...] += part

        def finish(off):
            gated = total_ref[:, :W] / total_ref[:, W:] * g_ref[row, off:off + span, :]
            update = jnp.dot(gated.astype(jnp.bfloat16), outw_ref[...], preferred_element_type=jnp.float32)
            base = base_ref[row, off:off + span, :].astype(jnp.float32)
            number = (off + lax.broadcasted_iota(jnp.int32, (span, 1), 0)).astype(jnp.float32)
            result = jnp.where((number < length) & inside, base + update, base)
            if first_module:
                done_ref[i, off:off + span, :] = result
            else:
                stage_ref[row, off:off + span, :] = result.astype(jnp.bfloat16)

        for stage in range(len(units) + 2):
            for t in range(len(tiles)):
                if stage < len(units):
                    score(stage, t)
                if stage >= 2:
                    combine(stage - 2, t)
                if 1 <= stage <= len(units):
                    soften(stage - 1, t)
            if stage >= 2 and units[stage - 2][1] == HEADS - 1:
                finish(units[stage - 2][0])

    if not first_module:
        def each_row(row, carry):
            one_row(row, None)
            for copy in row_copies(row):
                copy.start()
            return carry

        lax.fori_loop(0, rows, each_row, 0)
        for row in range(rows):
            remote, keep = row_copies(row)
            remote.wait()
            keep.wait()
        return

    mine_yc = lax.rem(me["y"], 2) * 4 + me["c"] * 2 + me["y"] // 2
    mine_xz = me["x"] * RING + me["z"]

    def first_copy(p, k):
        at = column[k]
        source = stage_ref.at[p, lax.rem(at["y"], 2), :, at["c"] * 2 + at["y"] // 2]
        goal = mail_ref.at[p, mine_yc]
        if k == 0:
            return pltpu.make_async_copy(source, goal, row_local.at[p])
        number = p * CORES * RING + k
        return pltpu.make_async_remote_copy(
            src_ref=source, dst_ref=goal, send_sem=row_send.at[number], recv_sem=row_recv.at[number],
            device_id=device_of(at), device_id_type=MESH,
        )

    def second_copy(p, k):
        at = level[k]
        source = mail_ref.at[p, :, at["x"] * RING + at["z"]]
        goal = out_ref.at[p, mine_xz]
        if k == 0:
            return pltpu.make_async_copy(source, goal, far_local.at[p])
        number = p * RING * RING + k
        return pltpu.make_async_remote_copy(
            src_ref=source, dst_ref=goal, send_sem=far_send.at[number], recv_sem=far_recv.at[number],
            device_id=device_of(at), device_id_type=MESH,
        )

    def pass_on(p):
        first_copy(p, 0).wait()
        for k in range(1, CORES * RING):
            first_copy(p, k).wait_recv()
        for k in range(RING * RING):
            second_copy(p, k).start()

    def each_pair(pair, carry):
        def one(i, inner):
            one_row(pair * 2 + i, i)
            return inner

        lax.fori_loop(0, 2, one, 0)
        both = [done_ref[i].reshape(n // rows, rows, -1) for i in range(2)]
        stage_ref[pair] = jnp.concatenate(both, axis=1).astype(jnp.bfloat16).reshape(stage_ref.shape[1:])
        for k in range(CORES * RING):
            first_copy(pair, k).start()

        @pl.when(pair > 0)
        def _():
            pass_on(pair - 1)

        return carry

    lax.fori_loop(0, steps, each_pair, 0)
    pass_on(steps - 1)
    for p in range(steps):
        for k in range(1, CORES * RING):
            first_copy(p, k).wait_send()
        second_copy(p, 0).wait()
        for k in range(1, RING * RING):
            second_copy(p, k).wait_send()
            second_copy(p, k).wait_recv()
    give_w.wait()


def module(source, mask, gain, w, bw, outw, *, first_module, n, rows, ident):
    c = source.shape[-1]
    steps = rows // 2
    yc, xz = CORES * RING, RING * RING
    shape = (rows, n, W)
    span = n // 2
    dma = pltpu.SemaphoreType.DMA
    scratch = [
        pltpu.VMEM((CORES, RING, RING, RING, HEADS * rows, n), jnp.bfloat16),
        pltpu.VMEM((HEADS, n, n), jnp.float32),
        pltpu.VMEM((rows, n, c), jnp.bfloat16),
        pltpu.VMEM(shape, jnp.bfloat16),
        pltpu.VMEM(shape, jnp.bfloat16),
        pltpu.VMEM(shape, jnp.bfloat16),
        pltpu.VMEM(shape, jnp.float32),
        pltpu.VMEM((HEADS, n, 2 * W), jnp.bfloat16),
        pltpu.VMEM((2, span, n), jnp.float32),
        pltpu.VMEM((2, span, n), jnp.bfloat16),
        pltpu.VMEM((span, 2 * W), jnp.float32),
        pltpu.VMEM((rows, n, c), jnp.bfloat16),
        pltpu.VMEM((HEADS * rows, n), jnp.float32),
        pltpu.VMEM((steps, 2, xz, yc // 2, 2 * rows, c) if first_module else (rows, n, c), jnp.bfloat16),
        dma((12,)), dma((12,)), dma((36,)), dma((36,)), dma((2,)),
    ]
    vmem = pl.BlockSpec(memory_space=pltpu.VMEM)
    hbm = pl.BlockSpec(memory_space=pl.ANY)
    if first_module:
        out_shape = [
            jax.ShapeDtypeStruct((steps, xz, yc, 2 * rows, c), jnp.bfloat16),
            jax.ShapeDtypeStruct((4, W, c), jnp.bfloat16),
            jax.ShapeDtypeStruct(bw.shape[1:], jnp.bfloat16),
        ]
        out_specs = [hbm, hbm, vmem]
        scratch += [
            dma((steps * yc,)), dma((steps * yc,)), dma((steps,)),
            pltpu.VMEM((2, n, c), jnp.float32),
            pltpu.VMEM((steps, yc, xz, 2 * rows, c), jnp.bfloat16),
            dma((steps * xz,)), dma((steps * xz,)), dma((steps,)),
            pltpu.VMEM((2, 4, W, c), jnp.bfloat16),
            pltpu.VMEM(bw.shape, jnp.bfloat16),
            dma((2,)), dma((2,)),
        ]
    else:
        out_shape = jax.ShapeDtypeStruct((2 * rows, n, c), jnp.bfloat16)
        out_specs = hbm
        scratch += [dma((rows,)), dma((rows,)), dma((rows,))]
    return pl.pallas_call(
        functools.partial(module_kernel, first_module=first_module, n=n, rows=rows),
        out_shape=out_shape,
        in_specs=[hbm if first_module else vmem] + [vmem] * 5,
        out_specs=out_specs,
        scratch_shapes=scratch,
        compiler_params=pltpu.CompilerParams(
            collective_id=ident, has_side_effects=True, vmem_limit_bytes=VMEM_LIMIT
        ),
    )(source, mask, gain, w, bw, outw)


def on_device(pair_map, residue_mask, gain_start, proj_start, bias_start, out_start, gain_end, proj_end, bias_end, out_end):
    n = pair_map.shape[1]
    rows = pair_map.shape[0] // 2
    rep = lax.axis_index("rep")
    mask = residue_mask[None, :]
    half = jnp.transpose(jnp.stack([proj_start, proj_end]), (0, 1, 3, 2))
    strip = jnp.transpose(jnp.stack([bias_start, bias_end]), (0, 2, 1))
    strip = lax.dynamic_update_slice_in_dim(
        jnp.zeros((2, 16, strip.shape[2]), strip.dtype), strip, rep * strip.shape[1], 1
    )
    inbox, w_end, strip_end = module(
        pair_map, mask, gain_start[None, :], half, strip, out_start, first_module=True, n=n, rows=rows, ident=0
    )
    return module(
        inbox, mask, gain_end[None, :], w_end, strip_end, out_end, first_module=False, n=n, rows=rows, ident=1
    )


def solution(mesh):
    in_specs = (
        P("dap", None, None), P(), P(), P(None, None, "rep"), P(None, "rep"), P(),
        P(), P(None, None, "rep"), P(None, "rep"), P(),
    )
    return jax.shard_map(on_device, mesh=mesh, in_specs=in_specs, out_specs=P("dap", None, None), check_vma=False)
```

```python
import functools
import math

import jax
import jax.numpy as jnp
from jax import lax
from jax.experimental import pallas as pl
from jax.experimental.pallas import tpu as pltpu
from jax.sharding import PartitionSpec as P

EPS = 1e-5
LOG2E = math.log2(math.e)
HEADS = 4
DH = 32
W = HEADS * DH
VMEM_LIMIT = 60 * 2**20
RING = 4
CORES = 2
MESH = pl.DeviceIdType.MESH


def place():
    dap, rep = lax.axis_index("dap"), lax.axis_index("rep")
    core = lax.rem(dap, CORES)
    z = lax.rem(dap // CORES, RING)
    x = lax.rem(dap // (CORES * RING), RING)
    y = rep * 2 + dap // (CORES * RING * RING)
    return {"c": core, "y": y, "x": x, "z": z}


def block_of(at):
    dap = ((lax.rem(at["y"], 2) * RING + at["x"]) * RING + at["z"]) * CORES + at["c"]
    return dap * 2 + at["y"] // 2


def device_of(at):
    dap = ((lax.rem(at["y"], 2) * RING + at["x"]) * RING + at["z"]) * CORES + at["c"]
    return {"dap": dap, "rep": at["y"] // 2}


def shifted(at, axis, by):
    size = CORES if axis == "c" else RING
    return {**at, axis: lax.rem(at[axis] + by + size, size)}


def normalize(floats, gain):
    center = jnp.mean(floats, axis=-1, keepdims=True)
    apart = floats - center
    spread = jnp.mean(apart * apart, axis=-1, keepdims=True)
    return (apart * lax.rsqrt(spread + EPS) * gain).astype(jnp.bfloat16)


ORDERS = ("xyz", "yzx", "zxy")
GRAIN = 64
TILES = 2


def gather_parts(n):
    unit = n // 8
    return ((0, 3 * unit), (3 * unit, 3 * unit), (6 * unit, 2 * unit))


def module_kernel(*refs, first_module, n, rows):
    if first_module:
        (map_ref, mask_ref, gain_ref, half_ref, strip_ref, outw_ref, out_ref, w_out, bw_out) = refs[:9]
        (gat_ref, bias_ref, norm_ref, q_ref, k_ref, v_ref, g_ref, vt_ref, score_ref, expo_ref, head_ref, top_ref, base_ref,
         own32, stage_ref, core_send, core_recv, send, recv, local_sem, row_send, row_recv, row_local,
         done_ref, mail_ref, far_send, far_recv, far_local, w_ref, strip_in, w_send, w_recv) = refs[9:]
    else:
        (map_ref, mask_ref, gain_ref, w_ref, bw_ref, outw_ref, out_ref) = refs[:7]
        (gat_ref, bias_ref, norm_ref, q_ref, k_ref, v_ref, g_ref, vt_ref, score_ref, expo_ref, head_ref, top_ref, base_ref,
         own32, stage_ref, core_send, core_recv, send, recv, local_sem, row_send, row_recv, row_local) = refs[7:]
    me = place()
    rep = lax.axis_index("rep")
    peer = shifted(me, "y", 2)
    row0 = block_of(me) * rows
    steps = rows // 2
    span = n // 2
    column = [{**me, "y": lax.rem(me["y"] + k // CORES, RING), "c": lax.rem(me["c"] + k % CORES, CORES)}
              for k in range(CORES * RING)]
    level = [{**me, "x": lax.rem(me["x"] + k // RING, RING), "z": lax.rem(me["z"] + k % RING, RING)}
             for k in range(RING * RING)]
    owner = lax.broadcasted_iota(jnp.int32, (W, 1), 0) // DH
    mask = mask_ref[...].astype(jnp.float32)
    length = jnp.sum(mask, axis=1, keepdims=True)
    valid = mask > 0.5

    if first_module:
        partners = column[1:] + level[1:]
    else:
        partners = [shifted(me, axis, by) for axis in "xyz" for by in (1, -1)] + [shifted(me, "c", 1), peer]
    barrier = pltpu.get_barrier_semaphore()
    for partner in partners:
        pl.semaphore_signal(barrier, inc=1, device_id=device_of(partner), device_id_type=MESH)

    started = []

    def push(src, dst, to, semaphores, number):
        copy = pltpu.make_async_remote_copy(
            src_ref=src, dst_ref=dst, send_sem=semaphores[0].at[number], recv_sem=semaphores[1].at[number],
            device_id=device_of(to), device_id_type=MESH,
        )
        copy.start()
        started.append(copy)
        return copy

    if first_module:
        fetch = pltpu.make_async_copy(map_ref.at[pl.ds(rep * rows, rows)], base_ref, local_sem.at[0])
        fetch.start()
        place_w = w_ref.at[:, :, pl.ds(rep * (W // 2), W // 2), :]
        keep_w = pltpu.make_async_copy(half_ref, place_w, local_sem.at[1])
        keep_w.start()
        pl.semaphore_wait(barrier, len(partners))
        strip_copy = push(strip_ref, strip_in, peer, (w_send, w_recv), 0)
        w_copy = push(half_ref, place_w, peer, (w_send, w_recv), 1)
        fetch.wait()
    else:
        four = 4 * rows * rows
        to = lax.broadcasted_iota(jnp.int32, (four, four), 0)
        come = lax.broadcasted_iota(jnp.int32, (four, four), 1)
        j, which, i = to // (4 * rows), (to // rows) % 4, to % rows
        turn = (come == ((i // 2 * 4 + which) * 2 + i % 2) * rows + j).astype(jnp.bfloat16)
        for low in range(2):
            for xz in range(RING * RING):
                piece = map_ref[:, xz, 4 * low:4 * low + 4].reshape(four, -1)
                result = jnp.dot(turn, piece, preferred_element_type=jnp.float32)
                first = (low * RING * RING + xz) * 4 * rows
                base_ref[:, first:first + 4 * rows, :] = result.reshape(rows, 4 * rows, -1).astype(jnp.bfloat16)

    def norm_row(i, carry):
        norm_ref[i] = normalize(base_ref[i].astype(jnp.float32), gain_ref[...])
        return carry

    lax.fori_loop(0, rows, norm_row, 0)
    if first_module:
        strip_copy.wait_recv()
        weights = strip_ref[0] + strip_in[0]
        later = strip_ref[1] + strip_in[1]
        bw_out[...] = later
    else:
        weights = bw_ref[...]

    def plane_row(i, carry):
        strip = lax.dot_general(weights, norm_ref[i], (((1,), (1,)), ((), ())), preferred_element_type=jnp.float32)
        for h in range(HEADS):
            own32[pl.ds(h * rows + i, 1), :] = strip[h:h + 1]
        return carry

    lax.fori_loop(0, rows, plane_row, 0)
    gat_ref[me["c"], me["y"], me["x"], me["z"]] = own32[...].astype(jnp.bfloat16)
    if not first_module:
        pl.semaphore_wait(barrier, len(partners))

    def project(i):
        normed = norm_ref[i]
        across = (w_ref[0, :3] if first_module else w_ref[:3]).reshape(3 * W, -1)
        down = w_ref[0, 3] if first_module else w_ref[3]
        both = (((1,), (1,)), ((), ()))
        turned = lax.dot_general(across, normed, both, preferred_element_type=jnp.float32)
        q_ref[i] = (turned[:W] * (DH**-0.5 * LOG2E)).astype(jnp.bfloat16)
        v_ref[i] = turned[W:2 * W].astype(jnp.bfloat16)
        g_ref[i] = jax.nn.sigmoid(turned[2 * W:])
        k_ref[i] = lax.dot_general(normed, down, both, preferred_element_type=jnp.float32).astype(jnp.bfloat16)

    def view(part, marks, half=None, split=None):
        first, width = gather_parts(n)[part]
        index = [me["c"]]
        for axis in "yxz":
            mark = marks[axis]
            if axis == split:
                index.append(pl.ds(2 * half, 2))
            elif mark is None:
                index.append(slice(None))
            else:
                index.append(mark)
        lines = pl.ds(16 * half, 16) if half is not None and split is None else slice(None)
        return gat_ref.at[(*index, lines, pl.ds(first, width))]

    def share(part, number, marks):
        area = view(part, marks)
        return push(area, area, shifted(me, "c", 1), (core_send, core_recv), part * 4 + number)

    def unfold(part, core, marks):
        first, width = gather_parts(n)[part]
        free = [axis for axis in "yxz" if marks[axis] is None]

        def one(t, carry):
            at = {**marks, free[0]: t // RING, free[1]: lax.rem(t, RING), "c": core}
            piece = gat_ref[core, at["y"], at["x"], at["z"], :, first:first + width].astype(jnp.float32)
            piece = jnp.where(valid[:, first:first + width], piece * LOG2E, -1e9)
            line = pl.multiple_of(block_of(at) * rows, rows)
            for h in range(HEADS):
                bias_ref[h, pl.ds(line, rows), first:first + width] = piece[h * rows:(h + 1) * rows]
            return carry

        lax.fori_loop(0, RING * RING, one, 0)

    sibling = shifted(me, "c", 1)["c"]
    pending = {}
    shared = {}
    sets = {}
    for phase in range(3):
        marks = {}
        for part, order in enumerate(ORDERS):
            axis = order[phase]
            marks[part] = {a: (None if a in order[:phase] else me[a]) for a in "yxz"}
            if phase > 0:
                for copy in pending[part]:
                    copy.wait_recv()
            area = view(part, marks[part])
            pending[part] = [
                push(area, area, shifted(me, axis, by), (send, recv), ((part * 3 + phase) * 2) * 2 + way)
                for way, by in enumerate((1, -1))
            ]
            if phase == 2:
                shared[part, 0] = share(part, 0, marks[part])
                sets[part, 0] = marks[part]
        if phase == 2:
            if first_module:
                keep_w.wait()
                w_copy.wait_recv()
            for i in range(4):
                project(i)
            for part in range(3):
                unfold(part, me["c"], sets[part, 0])
        for part, order in enumerate(ORDERS):
            axis = order[phase]
            split = order[0] if phase > 0 else None
            back = {**marks[part], axis: shifted(me, axis, -1)[axis]}
            ahead = {**marks[part], axis: shifted(me, axis, 1)[axis]}
            later_copies = []
            for way, (by, held) in enumerate(((1, back), (-1, ahead))):
                pending[part][way].wait_recv()
                area = view(part, held, half=way, split=split)
                later_copies.append(
                    push(area, area, shifted(me, axis, by), (send, recv), ((part * 3 + phase) * 2 + 1) * 2 + way)
                )
            if phase == 2:
                for number, held in ((1, back), (2, ahead)):
                    shared[part, number] = share(part, number, held)
                    sets[part, number] = held
            pending[part] = later_copies
    for i in range(4, rows):
        project(i)
    for part in range(3):
        for number in (1, 2):
            unfold(part, me["c"], sets[part, number])
        shared[part, 0].wait_recv()
        unfold(part, sibling, sets[part, 0])
    vt_ref[:, DH:, :] = jnp.ones((HEADS, 16, n), jnp.bfloat16)
    for part, order in enumerate(ORDERS):
        for copy in pending[part]:
            copy.wait_recv()
        axis = order[2]
        sets[part, 3] = {**{a: None for a in "yxz"}, axis: shifted(me, axis, 2)[axis]}
        shared[part, 3] = share(part, 3, sets[part, 3])
    for part in range(3):
        unfold(part, me["c"], sets[part, 3])
        for number in (1, 2):
            shared[part, number].wait_recv()
            unfold(part, sibling, sets[part, number])
    for part in range(3):
        shared[part, 3].wait_recv()
        unfold(part, sibling, sets[part, 3])
    for copy in started:
        copy.wait_send()
    if first_module:
        give_w = pltpu.make_async_copy(w_ref.at[1], w_out, local_sem.at[0])
        give_w.start()

    def flip(h, carry):
        side = 128
        for a in range(n // side):
            for b in range(a, n // side):
                rows_a, rows_b = slice(a * side, (a + 1) * side), slice(b * side, (b + 1) * side)
                upper = bias_ref[h, rows_a, rows_b]
                if a < b:
                    lower = bias_ref[h, rows_b, rows_a]
                    bias_ref[h, rows_a, rows_b] = lower.T
                bias_ref[h, rows_b, rows_a] = upper.T
        return carry

    lax.fori_loop(0, HEADS, flip, 0)

    units = [(off, h) for off in (0, span) for h in range(HEADS)]
    tile = n // TILES

    def row_copies(row, off):
        source = stage_ref.at[row, pl.ds(off, span)]
        goal = out_ref.at[rep * rows + row, pl.ds(off, span)]
        number = row * 2 + off // span
        remote = pltpu.make_async_remote_copy(
            src_ref=source, dst_ref=goal, send_sem=row_send.at[number], recv_sem=row_recv.at[number],
            device_id=device_of(peer), device_id_type=MESH,
        )
        return remote, pltpu.make_async_copy(source, goal, row_local.at[number])

    def one_row(row, i):
        inside = (row0 + row).astype(jnp.float32) < length
        for h in range(HEADS):
            vt_ref[h, :DH, :] = v_ref[row, h * DH:(h + 1) * DH, :]

        def score(unit, t):
            off, h = units[unit]
            keys = slice(t * tile, (t + 1) * tile)
            queries = q_ref[row, :, off:off + span]
            own = jnp.where(owner == h, queries, jnp.zeros_like(queries))
            scores = jnp.dot(k_ref[row, keys, :], own, preferred_element_type=jnp.float32)
            scores = scores + bias_ref[h, keys, off:off + span]
            top = jnp.max(scores, axis=0, keepdims=True)
            top_ref[unit % 2] = top if t == 0 else jnp.maximum(top, top_ref[unit % 2])
            score_ref[unit % 2, keys, :] = scores

        def soften(unit, t):
            for first in range(t * tile, (t + 1) * tile, GRAIN):
                keys = slice(first, first + GRAIN)
                expo = jnp.exp2(score_ref[unit % 2, keys, :] - top_ref[unit % 2])
                expo_ref[unit % 2, keys, :] = expo.astype(jnp.bfloat16)

        def combine(unit, t):
            h = units[unit][1]
            some = slice(t * (span // TILES), (t + 1) * (span // TILES))
            result = jnp.dot(vt_ref[h], expo_ref[unit % 2, :, some], preferred_element_type=jnp.float32)
            head_ref[h * DH:(h + 1) * DH, some] = result[:DH] / result[DH:DH + 1]

        def finish(off):
            gated = (head_ref[...] * g_ref[row, :, off:off + span]).astype(jnp.bfloat16)
            update = lax.dot_general(
                gated, outw_ref[...], (((0,), (0,)), ((), ())), preferred_element_type=jnp.float32
            )
            base = base_ref[row, off:off + span, :].astype(jnp.float32)
            number = (off + lax.broadcasted_iota(jnp.int32, (span, 1), 0)).astype(jnp.float32)
            result = jnp.where((number < length) & inside, base + update, base)
            if first_module:
                done_ref[i, off:off + span, :] = result
            else:
                stage_ref[row, off:off + span, :] = result.astype(jnp.bfloat16)
                for copy in row_copies(row, off):
                    copy.start()

        for stage in range(len(units) + 2):
            for t in range(TILES):
                if stage < len(units):
                    score(stage, t)
                if stage >= 2:
                    combine(stage - 2, t)
                if 1 <= stage <= len(units):
                    soften(stage - 1, t)
            if stage >= 2 and units[stage - 2][1] == HEADS - 1:
                finish(units[stage - 2][0])

    if not first_module:
        def each_row(row, carry):
            one_row(row, None)
            return carry

        lax.fori_loop(0, rows, each_row, 0)
        for row in range(rows):
            for off in (0, span):
                remote, keep = row_copies(row, off)
                remote.wait()
                keep.wait()
        return

    mine_yc = lax.rem(me["y"], 2) * 4 + me["c"] * 2 + me["y"] // 2
    mine_xz = me["x"] * RING + me["z"]

    def first_copy(p, k):
        at = column[k]
        source = stage_ref.at[p, lax.rem(at["y"], 2), :, at["c"] * 2 + at["y"] // 2]
        goal = mail_ref.at[p, mine_yc]
        if k == 0:
            return pltpu.make_async_copy(source, goal, row_local.at[p])
        number = p * CORES * RING + k
        return pltpu.make_async_remote_copy(
            src_ref=source, dst_ref=goal, send_sem=row_send.at[number], recv_sem=row_recv.at[number],
            device_id=device_of(at), device_id_type=MESH,
        )

    def second_copy(p, k):
        at = level[k]
        source = mail_ref.at[p, :, at["x"] * RING + at["z"]]
        goal = out_ref.at[p, mine_xz]
        if k == 0:
            return pltpu.make_async_copy(source, goal, far_local.at[p])
        number = p * RING * RING + k
        return pltpu.make_async_remote_copy(
            src_ref=source, dst_ref=goal, send_sem=far_send.at[number], recv_sem=far_recv.at[number],
            device_id=device_of(at), device_id_type=MESH,
        )

    def pass_on(p):
        first_copy(p, 0).wait()
        for k in range(1, CORES * RING):
            first_copy(p, k).wait_recv()
        for k in range(RING * RING):
            second_copy(p, k).start()

    def each_pair(pair, carry):
        def one(i, inner):
            one_row(pair * 2 + i, i)
            return inner

        lax.fori_loop(0, 2, one, 0)
        both = [done_ref[i].reshape(n // rows, rows, -1) for i in range(2)]
        stage_ref[pair] = jnp.concatenate(both, axis=1).astype(jnp.bfloat16).reshape(stage_ref.shape[1:])
        for k in range(CORES * RING):
            first_copy(pair, k).start()

        @pl.when(pair > 0)
        def _():
            pass_on(pair - 1)

        return carry

    lax.fori_loop(0, steps, each_pair, 0)
    pass_on(steps - 1)
    for p in range(steps):
        for k in range(1, CORES * RING):
            first_copy(p, k).wait_send()
        second_copy(p, 0).wait()
        for k in range(1, RING * RING):
            second_copy(p, k).wait_send()
            second_copy(p, k).wait_recv()
    give_w.wait()


def module(source, mask, gain, w, bw, outw, *, first_module, n, rows, ident):
    c = source.shape[-1]
    steps = rows // 2
    yc, xz = CORES * RING, RING * RING
    span = n // 2
    dma = pltpu.SemaphoreType.DMA
    scratch = [
        pltpu.VMEM((CORES, RING, RING, RING, HEADS * rows, n), jnp.bfloat16),
        pltpu.VMEM((HEADS, n, n), jnp.float32),
        pltpu.VMEM((rows, n, c), jnp.bfloat16),
        pltpu.VMEM((rows, W, n), jnp.bfloat16),
        pltpu.VMEM((rows, n, W), jnp.bfloat16),
        pltpu.VMEM((rows, W, n), jnp.bfloat16),
        pltpu.VMEM((rows, W, n), jnp.float32),
        pltpu.VMEM((HEADS, DH + 16, n), jnp.bfloat16),
        pltpu.VMEM((2, n, span), jnp.float32),
        pltpu.VMEM((2, n, span), jnp.bfloat16),
        pltpu.VMEM((W, span), jnp.float32),
        pltpu.VMEM((2, 1, span), jnp.float32),
        pltpu.VMEM((rows, n, c), jnp.bfloat16),
        pltpu.VMEM((HEADS * rows, n), jnp.float32),
        pltpu.VMEM((steps, 2, xz, yc // 2, 2 * rows, c) if first_module else (rows, n, c), jnp.bfloat16),
        dma((12,)), dma((12,)), dma((36,)), dma((36,)), dma((2,)),
    ]
    vmem = pl.BlockSpec(memory_space=pltpu.VMEM)
    hbm = pl.BlockSpec(memory_space=pl.ANY)
    if first_module:
        out_shape = [
            jax.ShapeDtypeStruct((steps, xz, yc, 2 * rows, c), jnp.bfloat16),
            jax.ShapeDtypeStruct((4, W, c), jnp.bfloat16),
            jax.ShapeDtypeStruct(bw.shape[1:], jnp.bfloat16),
        ]
        out_specs = [hbm, hbm, vmem]
        scratch += [
            dma((steps * yc,)), dma((steps * yc,)), dma((steps,)),
            pltpu.VMEM((2, n, c), jnp.float32),
            pltpu.VMEM((steps, yc, xz, 2 * rows, c), jnp.bfloat16),
            dma((steps * xz,)), dma((steps * xz,)), dma((steps,)),
            pltpu.VMEM((2, 4, W, c), jnp.bfloat16),
            pltpu.VMEM(bw.shape, jnp.bfloat16),
            dma((2,)), dma((2,)),
        ]
    else:
        out_shape = jax.ShapeDtypeStruct((2 * rows, n, c), jnp.bfloat16)
        out_specs = hbm
        scratch += [dma((2 * rows,)), dma((2 * rows,)), dma((2 * rows,))]
    return pl.pallas_call(
        functools.partial(module_kernel, first_module=first_module, n=n, rows=rows),
        out_shape=out_shape,
        in_specs=[hbm if first_module else vmem] + [vmem] * 5,
        out_specs=out_specs,
        scratch_shapes=scratch,
        compiler_params=pltpu.CompilerParams(
            collective_id=ident, has_side_effects=True, vmem_limit_bytes=VMEM_LIMIT
        ),
    )(source, mask, gain, w, bw, outw)


def on_device(pair_map, residue_mask, gain_start, proj_start, bias_start, out_start, gain_end, proj_end, bias_end, out_end):
    n = pair_map.shape[1]
    rows = pair_map.shape[0] // 2
    rep = lax.axis_index("rep")
    mask = residue_mask[None, :]
    half = jnp.stack([proj[f] for proj in (proj_start, proj_end) for f in (0, 2, 3, 1)])
    half = jnp.transpose(half.reshape(2, 4, *half.shape[1:]), (0, 1, 3, 2))
    strip = jnp.transpose(jnp.stack([bias_start, bias_end]), (0, 2, 1))
    strip = lax.dynamic_update_slice_in_dim(
        jnp.zeros((2, 16, strip.shape[2]), strip.dtype), strip, rep * strip.shape[1], 1
    )
    inbox, w_end, strip_end = module(
        pair_map, mask, gain_start[None, :], half, strip, out_start, first_module=True, n=n, rows=rows, ident=0
    )
    return module(
        inbox, mask, gain_end[None, :], w_end, strip_end, out_end, first_module=False, n=n, rows=rows, ident=1
    )


def solution(mesh):
    in_specs = (
        P("dap", None, None), P(), P(), P(None, None, "rep"), P(None, "rep"), P(),
        P(), P(None, None, "rep"), P(None, "rep"), P(),
    )
    return jax.shard_map(on_device, mesh=mesh, in_specs=in_specs, out_specs=P("dap", None, None), check_vma=False)
```

```python
import functools
import math

import jax
import jax.numpy as jnp
from jax import lax
from jax.experimental import pallas as pl
from jax.experimental.pallas import tpu as pltpu
from jax.sharding import PartitionSpec as P

EPS = 1e-5
LOG2E = math.log2(math.e)
HEADS = 4
DH = 32
W = HEADS * DH
VMEM_LIMIT = 60 * 2**20
RING = 4
CORES = 2
MESH = pl.DeviceIdType.MESH


def place():
    dap, rep = lax.axis_index("dap"), lax.axis_index("rep")
    core = lax.rem(dap, CORES)
    z = lax.rem(dap // CORES, RING)
    x = lax.rem(dap // (CORES * RING), RING)
    y = rep * 2 + dap // (CORES * RING * RING)
    return {"c": core, "y": y, "x": x, "z": z}


def block_of(at):
    dap = ((lax.rem(at["y"], 2) * RING + at["x"]) * RING + at["z"]) * CORES + at["c"]
    return dap * 2 + at["y"] // 2


def device_of(at):
    dap = ((lax.rem(at["y"], 2) * RING + at["x"]) * RING + at["z"]) * CORES + at["c"]
    return {"dap": dap, "rep": at["y"] // 2}


def shifted(at, axis, by):
    size = CORES if axis == "c" else RING
    return {**at, axis: lax.rem(at[axis] + by + size, size)}


def normalize(floats, gain):
    center = jnp.mean(floats, axis=-1, keepdims=True)
    apart = floats - center
    spread = jnp.mean(apart * apart, axis=-1, keepdims=True)
    return (apart * lax.rsqrt(spread + EPS) * gain).astype(jnp.bfloat16)


ORDERS = ("xyz", "yzx", "zxy")
GRAIN = 64
TILES = 2


def gather_parts(n):
    unit = n // 8
    return ((0, 3 * unit), (3 * unit, 3 * unit), (6 * unit, 2 * unit))


def module_kernel(*refs, first_module, n, rows):
    if first_module:
        (map_ref, mask_ref, gain_ref, half_ref, strip_ref, outw_ref, out_ref, w_out, bw_out) = refs[:9]
        (gat_ref, bias_ref, norm_ref, q_ref, k_ref, v_ref, g_ref, vt_ref, score_ref, expo_ref, head_ref, top_ref, base_ref,
         own32, stage_ref, core_send, core_recv, send, recv, local_sem, row_send, row_recv, row_local,
         done_ref, mail_ref, far_send, far_recv, far_local, w_ref, strip_in, w_send, w_recv) = refs[9:]
    else:
        (map_ref, mask_ref, gain_ref, w_ref, bw_ref, outw_ref, out_ref) = refs[:7]
        (gat_ref, bias_ref, norm_ref, q_ref, k_ref, v_ref, g_ref, vt_ref, score_ref, expo_ref, head_ref, top_ref, base_ref,
         own32, stage_ref, core_send, core_recv, send, recv, local_sem, row_send, row_recv, row_local, more_send, more_recv) = refs[7:]
    me = place()
    rep = lax.axis_index("rep")
    peer = shifted(me, "y", 2)
    row0 = block_of(me) * rows
    steps = rows // 2
    span = n // 2
    column = [{**me, "y": lax.rem(me["y"] + k // CORES, RING), "c": lax.rem(me["c"] + k % CORES, CORES)}
              for k in range(CORES * RING)]
    level = [{**me, "x": lax.rem(me["x"] + k // RING, RING), "z": lax.rem(me["z"] + k % RING, RING)}
             for k in range(RING * RING)]
    owner = lax.broadcasted_iota(jnp.int32, (W, 1), 0) // DH
    mask = mask_ref[...].astype(jnp.float32)
    length = jnp.sum(mask, axis=1, keepdims=True)
    valid = mask > 0.5

    if first_module:
        partners = column[1:] + level[1:]
    else:
        partners = [shifted(me, axis, by) for axis in "xyz" for by in (1, -1)] + [shifted(me, "c", 1), peer]
    barrier = pltpu.get_barrier_semaphore()
    for partner in partners:
        pl.semaphore_signal(barrier, inc=1, device_id=device_of(partner), device_id_type=MESH)

    started = []

    def push(src, dst, to, semaphores, number):
        copy = pltpu.make_async_remote_copy(
            src_ref=src, dst_ref=dst, send_sem=semaphores[0].at[number], recv_sem=semaphores[1].at[number],
            device_id=device_of(to), device_id_type=MESH,
        )
        copy.start()
        started.append(copy)
        return copy

    if first_module:
        fetch = pltpu.make_async_copy(map_ref.at[pl.ds(rep * rows, rows)], base_ref, local_sem.at[0])
        fetch.start()
        place_w = w_ref.at[:, :, pl.ds(rep * (W // 2), W // 2), :]
        keep_w = pltpu.make_async_copy(half_ref, place_w, local_sem.at[1])
        keep_w.start()
        pl.semaphore_wait(barrier, len(partners))
        strip_copy = push(strip_ref, strip_in, peer, (w_send, w_recv), 0)
        w_copy = push(half_ref, place_w, peer, (w_send, w_recv), 1)
        fetch.wait()
    else:
        four = 4 * rows * rows
        to = lax.broadcasted_iota(jnp.int32, (four, four), 0)
        come = lax.broadcasted_iota(jnp.int32, (four, four), 1)
        j, which, i = to // (4 * rows), (to // rows) % 4, to % rows
        turn = (come == ((i // 2 * 4 + which) * 2 + i % 2) * rows + j).astype(jnp.bfloat16)
        for low in range(2):
            for xz in range(RING * RING):
                piece = map_ref[:, xz, 4 * low:4 * low + 4].reshape(four, -1)
                result = jnp.dot(turn, piece, preferred_element_type=jnp.float32)
                first = (low * RING * RING + xz) * 4 * rows
                base_ref[:rows, first:first + 4 * rows, :] = result.reshape(rows, 4 * rows, -1).astype(jnp.bfloat16)

        pl.semaphore_wait(barrier, len(partners))
        more = push(base_ref.at[rows - 1], base_ref.at[rows], peer, (more_send, more_recv), 0)

    def norm_row(i):
        norm_ref[i] = normalize(base_ref[i].astype(jnp.float32), gain_ref[...])

    for i in range(rows):
        norm_row(i)
    if first_module:
        strip_copy.wait_recv()
        weights = strip_ref[0] + strip_in[0]
        later = strip_ref[1] + strip_in[1]
        bw_out[...] = later
    else:
        weights = bw_ref[...]

    for i in range(rows):
        strip = lax.dot_general(weights, norm_ref[i], (((1,), (1,)), ((), ())), preferred_element_type=jnp.float32)
        for h in range(HEADS):
            own32[h * rows + i:h * rows + i + 1, :] = strip[h:h + 1]

    gat_ref[me["c"], me["y"], me["x"], me["z"]] = own32[...].astype(jnp.bfloat16)
    def project(i):
        normed = norm_ref[i]
        weights = w_ref[0] if first_module else w_ref[...]
        both = (((1,), (1,)), ((), ()))
        queries = lax.dot_general(weights[0], normed, both, preferred_element_type=jnp.float32)
        q_ref[i] = (queries * (DH**-0.5 * LOG2E)).astype(jnp.bfloat16)
        rest = lax.dot_general(weights[2:].reshape(2 * W, -1), normed, both, preferred_element_type=jnp.float32)
        v_ref[i] = rest[:W].astype(jnp.bfloat16)
        g_ref[i] = jax.nn.sigmoid(rest[W:])
        k_ref[i] = lax.dot_general(normed, weights[1], both, preferred_element_type=jnp.float32).astype(jnp.bfloat16)

    def view(part, marks, half=None, split=None):
        first, width = gather_parts(n)[part]
        index = [me["c"]]
        for axis in "yxz":
            mark = marks[axis]
            if axis == split:
                index.append(pl.ds(2 * half, 2))
            elif mark is None:
                index.append(slice(None))
            else:
                index.append(mark)
        lines = pl.ds(16 * half, 16) if half is not None and split is None else slice(None)
        return gat_ref.at[(*index, lines, pl.ds(first, width))]

    def share(part, number, marks):
        area = view(part, marks)
        return push(area, area, shifted(me, "c", 1), (core_send, core_recv), part * 4 + number)

    def unfold(part, core, marks):
        first, width = gather_parts(n)[part]
        free = [axis for axis in "yxz" if marks[axis] is None]

        def one(t, carry):
            at = {**marks, free[0]: t // RING, free[1]: lax.rem(t, RING), "c": core}
            piece = gat_ref[core, at["y"], at["x"], at["z"], :, first:first + width].astype(jnp.float32)
            piece = jnp.where(valid[:, first:first + width], piece * LOG2E, -1e9)
            line = pl.multiple_of(block_of(at) * rows, rows)
            for h in range(HEADS):
                bias_ref[h, pl.ds(line, rows), first:first + width] = piece[h * rows:(h + 1) * rows]
            return carry

        lax.fori_loop(0, RING * RING, one, 0)

    sibling = shifted(me, "c", 1)["c"]
    pending = {}
    shared = {}
    sets = {}
    for phase in range(3):
        marks = {}
        for part, order in enumerate(ORDERS):
            axis = order[phase]
            marks[part] = {a: (None if a in order[:phase] else me[a]) for a in "yxz"}
            if phase > 0:
                for copy in pending[part]:
                    copy.wait_recv()
            split = order[0] if phase > 0 else None
            pending[part] = []
            for kind in range(2):
                for way, by in enumerate((1, -1)):
                    area = view(part, marks[part], half=kind ^ way, split=split)
                    number = ((part * 3 + phase) * 3 + kind) * 2 + way
                    pending[part].append(push(area, area, shifted(me, axis, by), (send, recv), number))
            if phase == 2:
                shared[part, 0] = share(part, 0, marks[part])
                sets[part, 0] = marks[part]
        if phase == 2:
            if first_module:
                keep_w.wait()
                w_copy.wait_recv()
            for i in range(4):
                project(i)
            for part in range(3):
                unfold(part, me["c"], sets[part, 0])
        for part, order in enumerate(ORDERS):
            axis = order[phase]
            split = order[0] if phase > 0 else None
            back = {**marks[part], axis: shifted(me, axis, -1)[axis]}
            ahead = {**marks[part], axis: shifted(me, axis, 1)[axis]}
            later_copies = []
            for way, (by, held) in enumerate(((1, back), (-1, ahead))):
                pending[part][way].wait_recv()
                area = view(part, held, half=way, split=split)
                later_copies.append(
                    push(area, area, shifted(me, axis, by), (send, recv), ((part * 3 + phase) * 3 + 2) * 2 + way)
                )
            sets[part, 1], sets[part, 2] = back, ahead
            pending[part] = pending[part][2:] + later_copies
        if phase == 2:
            for part in range(3):
                for copy in pending[part][:2]:
                    copy.wait_recv()
                pending[part] = pending[part][2:]
                for number in (1, 2):
                    shared[part, number] = share(part, number, sets[part, number])
    for i in range(4, rows):
        project(i)
    if not first_module:
        more.wait_recv()
        norm_row(rows)
        project(rows)
    for part in range(3):
        for number in (1, 2):
            unfold(part, me["c"], sets[part, number])
        shared[part, 0].wait_recv()
        unfold(part, sibling, sets[part, 0])
    vt_ref[:, DH:, :] = jnp.ones((HEADS, 16, n), jnp.bfloat16)
    for part, order in enumerate(ORDERS):
        for copy in pending[part]:
            copy.wait_recv()
        axis = order[2]
        sets[part, 3] = {**{a: None for a in "yxz"}, axis: shifted(me, axis, 2)[axis]}
        shared[part, 3] = share(part, 3, sets[part, 3])
    for part in range(3):
        unfold(part, me["c"], sets[part, 3])
        for number in (1, 2):
            shared[part, number].wait_recv()
            unfold(part, sibling, sets[part, number])
    for part in range(3):
        shared[part, 3].wait_recv()
        unfold(part, sibling, sets[part, 3])
    for copy in started:
        copy.wait_send()
    if first_module:
        give_w = pltpu.make_async_copy(w_ref.at[1], w_out, local_sem.at[0])
        give_w.start()

    def flip(h, carry):
        side = 128
        for a in range(n // side):
            for b in range(a, n // side):
                rows_a, rows_b = slice(a * side, (a + 1) * side), slice(b * side, (b + 1) * side)
                upper = bias_ref[h, rows_a, rows_b]
                if a < b:
                    lower = bias_ref[h, rows_b, rows_a]
                    bias_ref[h, rows_a, rows_b] = lower.T
                bias_ref[h, rows_b, rows_a] = upper.T
        return carry

    lax.fori_loop(0, HEADS, flip, 0)

    units = [(off, h) for off in (0, span) for h in range(HEADS)]
    tile = n // TILES

    def away(row):
        return (row // rows) * ((1 - 2 * rep) * rows - 1)

    def row_ends(row, off):
        return stage_ref.at[row, pl.ds(off, span)], out_ref.at[rep * rows + row + away(row), pl.ds(off, span)]

    def row_keep(row, off):
        source, goal = row_ends(row, off)
        return pltpu.make_async_copy(source, goal, row_local.at[row * 2 + off // span])

    def row_give(row, off):
        source, goal = row_ends(row, off)
        number = row * 2 + off // span
        return pltpu.make_async_remote_copy(
            src_ref=source, dst_ref=goal, send_sem=row_send.at[number], recv_sem=row_recv.at[number],
            device_id=device_of(peer), device_id_type=MESH,
        )

    def one_row(row, i):
        inside = (row0 + row + away(row)).astype(jnp.float32) < length
        for h in range(HEADS):
            vt_ref[h, :DH, :] = v_ref[row, h * DH:(h + 1) * DH, :]

        def score(unit, t):
            off, h = units[unit]
            keys = slice(t * tile, (t + 1) * tile)
            queries = q_ref[row, :, off:off + span]
            own = jnp.where(owner == h, queries, jnp.zeros_like(queries))
            scores = jnp.dot(k_ref[row, keys, :], own, preferred_element_type=jnp.float32)
            scores = scores + bias_ref[h, keys, off:off + span]
            top = jnp.max(scores, axis=0, keepdims=True)
            top_ref[unit % 2] = top if t == 0 else jnp.maximum(top, top_ref[unit % 2])
            score_ref[unit % 2, keys, :] = scores

        def soften(unit, t):
            for first in range(t * tile, (t + 1) * tile, GRAIN):
                keys = slice(first, first + GRAIN)
                expo = jnp.exp2(score_ref[unit % 2, keys, :] - top_ref[unit % 2])
                expo_ref[unit % 2, keys, :] = expo.astype(jnp.bfloat16)

        def combine(unit, t):
            h = units[unit][1]
            some = slice(t * (span // TILES), (t + 1) * (span // TILES))
            result = jnp.dot(vt_ref[h], expo_ref[unit % 2, :, some], preferred_element_type=jnp.float32)
            head_ref[h * DH:(h + 1) * DH, some] = result[:DH] / result[DH:DH + 1]

        def finish(off):
            gated = (head_ref[...] * g_ref[row, :, off:off + span]).astype(jnp.bfloat16)
            update = lax.dot_general(
                gated, outw_ref[...], (((0,), (0,)), ((), ())), preferred_element_type=jnp.float32
            )
            base = base_ref[row, off:off + span, :].astype(jnp.float32)
            number = (off + lax.broadcasted_iota(jnp.int32, (span, 1), 0)).astype(jnp.float32)
            result = jnp.where((number < length) & inside, base + update, base)
            if first_module:
                done_ref[i, off:off + span, :] = result
            else:
                stage_ref[row, off:off + span, :] = result.astype(jnp.bfloat16)
                row_keep(row, off).start()

                @pl.when(row < rows - 1)
                def _():
                    row_give(row, off).start()

        for stage in range(len(units) + 2):
            for t in range(TILES):
                if stage < len(units):
                    score(stage, t)
                if stage >= 2:
                    combine(stage - 2, t)
                if 1 <= stage <= len(units):
                    soften(stage - 1, t)
            if stage >= 2 and units[stage - 2][1] == HEADS - 1:
                finish(units[stage - 2][0])

    if not first_module:
        def each_row(row, carry):
            one_row(row, None)
            return carry

        lax.fori_loop(0, rows + 1, each_row, 0)
        for row in range(rows + 1):
            for off in (0, span):
                row_keep(row, off).wait()
                if row < rows - 1:
                    row_give(row, off).wait()
        return

    mine_yc = lax.rem(me["y"], 2) * 4 + me["c"] * 2 + me["y"] // 2
    mine_xz = me["x"] * RING + me["z"]

    def first_copy(p, k):
        at = column[k]
        source = stage_ref.at[p, lax.rem(at["y"], 2), :, at["c"] * 2 + at["y"] // 2]
        goal = mail_ref.at[p, mine_yc]
        if k == 0:
            return pltpu.make_async_copy(source, goal, row_local.at[p])
        number = p * CORES * RING + k
        return pltpu.make_async_remote_copy(
            src_ref=source, dst_ref=goal, send_sem=row_send.at[number], recv_sem=row_recv.at[number],
            device_id=device_of(at), device_id_type=MESH,
        )

    def second_copy(p, k):
        at = level[k]
        source = mail_ref.at[p, :, at["x"] * RING + at["z"]]
        goal = out_ref.at[p, mine_xz]
        if k == 0:
            return pltpu.make_async_copy(source, goal, far_local.at[p])
        number = p * RING * RING + k
        return pltpu.make_async_remote_copy(
            src_ref=source, dst_ref=goal, send_sem=far_send.at[number], recv_sem=far_recv.at[number],
            device_id=device_of(at), device_id_type=MESH,
        )

    def pass_on(p):
        first_copy(p, 0).wait()
        for k in range(1, CORES * RING):
            first_copy(p, k).wait_recv()
        for k in range(RING * RING):
            second_copy(p, k).start()

    def each_pair(pair, carry):
        def one(i, inner):
            one_row(pair * 2 + i, i)
            return inner

        lax.fori_loop(0, 2, one, 0)
        both = [done_ref[i].reshape(n // rows, rows, -1) for i in range(2)]
        stage_ref[pair] = jnp.concatenate(both, axis=1).astype(jnp.bfloat16).reshape(stage_ref.shape[1:])
        for k in range(CORES * RING):
            first_copy(pair, k).start()

        @pl.when(pair > 0)
        def _():
            pass_on(pair - 1)

        return carry

    lax.fori_loop(0, steps, each_pair, 0)
    pass_on(steps - 1)
    for p in range(steps):
        for k in range(1, CORES * RING):
            first_copy(p, k).wait_send()
        second_copy(p, 0).wait()
        for k in range(1, RING * RING):
            second_copy(p, k).wait_send()
            second_copy(p, k).wait_recv()
    give_w.wait()


def module(source, mask, gain, w, bw, outw, *, first_module, n, rows, ident):
    c = source.shape[-1]
    steps = rows // 2
    yc, xz = CORES * RING, RING * RING
    span = n // 2
    held = rows if first_module else rows + 1
    dma = pltpu.SemaphoreType.DMA
    scratch = [
        pltpu.VMEM((CORES, RING, RING, RING, HEADS * rows, n), jnp.bfloat16),
        pltpu.VMEM((HEADS, n, n), jnp.float32),
        pltpu.VMEM((held, n, c), jnp.bfloat16),
        pltpu.VMEM((held, W, n), jnp.bfloat16),
        pltpu.VMEM((held, n, W), jnp.bfloat16),
        pltpu.VMEM((held, W, n), jnp.bfloat16),
        pltpu.VMEM((held, W, n), jnp.float32),
        pltpu.VMEM((HEADS, DH + 16, n), jnp.bfloat16),
        pltpu.VMEM((2, n, span), jnp.float32),
        pltpu.VMEM((2, n, span), jnp.bfloat16),
        pltpu.VMEM((W, span), jnp.float32),
        pltpu.VMEM((2, 1, span), jnp.float32),
        pltpu.VMEM((held, n, c), jnp.bfloat16),
        pltpu.VMEM((HEADS * rows, n), jnp.float32),
        pltpu.VMEM((steps, 2, xz, yc // 2, 2 * rows, c) if first_module else (held, n, c), jnp.bfloat16),
        dma((12,)), dma((12,)), dma((54,)), dma((54,)), dma((2,)),
    ]
    vmem = pl.BlockSpec(memory_space=pltpu.VMEM)
    hbm = pl.BlockSpec(memory_space=pl.ANY)
    if first_module:
        out_shape = [
            jax.ShapeDtypeStruct((steps, xz, yc, 2 * rows, c), jnp.bfloat16),
            jax.ShapeDtypeStruct((4, W, c), jnp.bfloat16),
            jax.ShapeDtypeStruct(bw.shape[1:], jnp.bfloat16),
        ]
        out_specs = [hbm, hbm, vmem]
        scratch += [
            dma((steps * yc,)), dma((steps * yc,)), dma((steps,)),
            pltpu.VMEM((2, n, c), jnp.float32),
            pltpu.VMEM((steps, yc, xz, 2 * rows, c), jnp.bfloat16),
            dma((steps * xz,)), dma((steps * xz,)), dma((steps,)),
            pltpu.VMEM((2, 4, W, c), jnp.bfloat16),
            pltpu.VMEM(bw.shape, jnp.bfloat16),
            dma((2,)), dma((2,)),
        ]
    else:
        out_shape = jax.ShapeDtypeStruct((2 * rows, n, c), jnp.bfloat16)
        out_specs = hbm
        scratch += [dma((2 * held,)), dma((2 * held,)), dma((2 * held,)), dma((1,)), dma((1,))]
    return pl.pallas_call(
        functools.partial(module_kernel, first_module=first_module, n=n, rows=rows),
        out_shape=out_shape,
        in_specs=[hbm if first_module else vmem] + [vmem] * 5,
        out_specs=out_specs,
        scratch_shapes=scratch,
        compiler_params=pltpu.CompilerParams(
            collective_id=ident, has_side_effects=True, vmem_limit_bytes=VMEM_LIMIT
        ),
    )(source, mask, gain, w, bw, outw)


def on_device(pair_map, residue_mask, gain_start, proj_start, bias_start, out_start, gain_end, proj_end, bias_end, out_end):
    n = pair_map.shape[1]
    rows = pair_map.shape[0] // 2
    rep = lax.axis_index("rep")
    mask = residue_mask[None, :]
    half = jnp.transpose(jnp.stack([proj_start, proj_end]), (0, 1, 3, 2))
    strip = jnp.transpose(jnp.stack([bias_start, bias_end]), (0, 2, 1))
    strip = lax.dynamic_update_slice_in_dim(
        jnp.zeros((2, 16, strip.shape[2]), strip.dtype), strip, rep * strip.shape[1], 1
    )
    inbox, w_end, strip_end = module(
        pair_map, mask, gain_start[None, :], half, strip, out_start, first_module=True, n=n, rows=rows, ident=0
    )
    return module(
        inbox, mask, gain_end[None, :], w_end, strip_end, out_end, first_module=False, n=n, rows=rows, ident=1
    )


def solution(mesh):
    in_specs = (
        P("dap", None, None), P(), P(), P(None, None, "rep"), P(None, "rep"), P(),
        P(), P(None, None, "rep"), P(None, "rep"), P(),
    )
    return jax.shard_map(on_device, mesh=mesh, in_specs=in_specs, out_specs=P("dap", None, None), check_vma=False)
```

```python
import functools
import math

import jax
import jax.numpy as jnp
from jax import lax
from jax.experimental import pallas as pl
from jax.experimental.pallas import tpu as pltpu
from jax.sharding import PartitionSpec as P

EPS = 1e-5
LOG2E = math.log2(math.e)
HEADS = 4
DH = 32
W = HEADS * DH
VMEM_LIMIT = 60 * 2**20
RING = 4
CORES = 2
MESH = pl.DeviceIdType.MESH


def place():
    dap, rep = lax.axis_index("dap"), lax.axis_index("rep")
    core = lax.rem(dap, CORES)
    z = lax.rem(dap // CORES, RING)
    x = lax.rem(dap // (CORES * RING), RING)
    y = rep * 2 + dap // (CORES * RING * RING)
    return {"c": core, "y": y, "x": x, "z": z}


def block_of(at):
    dap = ((lax.rem(at["y"], 2) * RING + at["x"]) * RING + at["z"]) * CORES + at["c"]
    return dap * 2 + at["y"] // 2


def device_of(at):
    dap = ((lax.rem(at["y"], 2) * RING + at["x"]) * RING + at["z"]) * CORES + at["c"]
    return {"dap": dap, "rep": at["y"] // 2}


def shifted(at, axis, by):
    size = CORES if axis == "c" else RING
    return {**at, axis: lax.rem(at[axis] + by + size, size)}


def normalize(floats, gain):
    center = jnp.mean(floats, axis=-1, keepdims=True)
    apart = floats - center
    spread = jnp.mean(apart * apart, axis=-1, keepdims=True)
    return (apart * lax.rsqrt(spread + EPS) * gain).astype(jnp.bfloat16)


ORDERS = ("xyz", "yzx", "zxy")
GRAIN = 64
TILES = 2


def gather_parts(n):
    unit = n // 8
    return ((0, 3 * unit), (3 * unit, 3 * unit), (6 * unit, 2 * unit))


def module_kernel(*refs, first_module, n, rows):
    if first_module:
        (map_ref, mask_ref, gain_ref, half_ref, strip_ref, outw_ref, out_ref, w_out, bw_out) = refs[:9]
        (gat_ref, bias_ref, norm_ref, q_ref, k_ref, v_ref, g_ref, vt_ref, score_ref, expo_ref, head_ref, top_ref, base_ref,
         own32, stage_ref, core_send, core_recv, send, recv, local_sem, row_send, row_recv, row_local,
         done_ref, mail_ref, far_send, far_recv, far_local, w_ref, strip_in, w_send, w_recv) = refs[9:]
    else:
        (map_ref, mask_ref, gain_ref, w_ref, bw_ref, outw_ref, out_ref) = refs[:7]
        (gat_ref, bias_ref, norm_ref, q_ref, k_ref, v_ref, g_ref, vt_ref, score_ref, expo_ref, head_ref, top_ref, base_ref,
         own32, stage_ref, core_send, core_recv, send, recv, local_sem, row_send, row_recv, row_local, more_send, more_recv) = refs[7:]
    me = place()
    rep = lax.axis_index("rep")
    peer = shifted(me, "y", 2)
    row0 = block_of(me) * rows
    steps = rows // 2
    span = n // 2
    column = [{**me, "y": lax.rem(me["y"] + k // CORES, RING), "c": lax.rem(me["c"] + k % CORES, CORES)}
              for k in range(CORES * RING)]
    level = [{**me, "x": lax.rem(me["x"] + k // RING, RING), "z": lax.rem(me["z"] + k % RING, RING)}
             for k in range(RING * RING)]
    owner = lax.broadcasted_iota(jnp.int32, (W, 1), 0) // DH
    mask = mask_ref[...].astype(jnp.float32)
    length = jnp.sum(mask, axis=1, keepdims=True)
    valid = mask > 0.5

    if first_module:
        partners = column[1:] + level[1:]
    else:
        partners = [shifted(me, axis, by) for axis in "xyz" for by in (1, -1, 2)] + [shifted(me, "c", 1)]
    barrier = pltpu.get_barrier_semaphore()
    for partner in partners:
        pl.semaphore_signal(barrier, inc=1, device_id=device_of(partner), device_id_type=MESH)

    started = []

    def push(src, dst, to, semaphores, number):
        copy = pltpu.make_async_remote_copy(
            src_ref=src, dst_ref=dst, send_sem=semaphores[0].at[number], recv_sem=semaphores[1].at[number],
            device_id=device_of(to), device_id_type=MESH,
        )
        copy.start()
        started.append(copy)
        return copy

    if first_module:
        fetch = pltpu.make_async_copy(map_ref.at[pl.ds(rep * rows, rows)], base_ref, local_sem.at[0])
        fetch.start()
        place_w = w_ref.at[:, :, pl.ds(rep * (W // 2), W // 2), :]
        keep_w = pltpu.make_async_copy(half_ref, place_w, local_sem.at[1])
        keep_w.start()
        pl.semaphore_wait(barrier, len(partners))
        strip_copy = push(strip_ref, strip_in, peer, (w_send, w_recv), 0)
        w_copy = push(half_ref, place_w, peer, (w_send, w_recv), 1)
        fetch.wait()
    else:
        four = 4 * rows * rows
        to = lax.broadcasted_iota(jnp.int32, (four, four), 0)
        come = lax.broadcasted_iota(jnp.int32, (four, four), 1)
        j, which, i = to // (4 * rows), (to // rows) % 4, to % rows
        turn = (come == ((i // 2 * 4 + which) * 2 + i % 2) * rows + j).astype(jnp.bfloat16)
        for low in range(2):
            for xz in range(RING * RING):
                piece = map_ref[:, xz, 4 * low:4 * low + 4].reshape(four, -1)
                result = jnp.dot(turn, piece, preferred_element_type=jnp.float32)
                first = (low * RING * RING + xz) * 4 * rows
                base_ref[:rows, first:first + 4 * rows, :] = result.reshape(rows, 4 * rows, -1).astype(jnp.bfloat16)

        pl.semaphore_wait(barrier, len(partners))
        more = push(base_ref.at[rows - 1], base_ref.at[rows], peer, (more_send, more_recv), 0)

    def norm_row(i):
        norm_ref[i] = normalize(base_ref[i].astype(jnp.float32), gain_ref[...])

    for i in range(rows):
        norm_row(i)
    if first_module:
        strip_copy.wait_recv()
        weights = strip_ref[0] + strip_in[0]
        later = strip_ref[1] + strip_in[1]
        bw_out[...] = later
    else:
        weights = bw_ref[...]

    for i in range(rows):
        strip = lax.dot_general(weights, norm_ref[i], (((1,), (1,)), ((), ())), preferred_element_type=jnp.float32)
        for h in range(HEADS):
            own32[h * rows + i:h * rows + i + 1, :] = strip[h:h + 1]

    gat_ref[me["c"], me["y"], me["x"], me["z"]] = own32[...].astype(jnp.bfloat16)
    def project(i):
        normed = norm_ref[i]
        weights = w_ref[0] if first_module else w_ref[...]
        both = (((1,), (1,)), ((), ()))
        queries = lax.dot_general(weights[0], normed, both, preferred_element_type=jnp.float32)
        q_ref[i] = (queries * (DH**-0.5 * LOG2E)).astype(jnp.bfloat16)
        rest = lax.dot_general(weights[2:].reshape(2 * W, -1), normed, both, preferred_element_type=jnp.float32)
        v_ref[i] = rest[:W].astype(jnp.bfloat16)
        g_ref[i] = jax.nn.sigmoid(rest[W:])
        k_ref[i] = lax.dot_general(normed, weights[1], both, preferred_element_type=jnp.float32).astype(jnp.bfloat16)

    def view(part, marks, half=None, split=None):
        first, width = gather_parts(n)[part]
        index = [me["c"]]
        for axis in "yxz":
            mark = marks[axis]
            if axis == split:
                index.append(pl.ds(2 * half, 2))
            elif mark is None:
                index.append(slice(None))
            else:
                index.append(mark)
        lines = pl.ds(16 * half, 16) if half is not None and split is None else slice(None)
        return gat_ref.at[(*index, lines, pl.ds(first, width))]

    def share(part, number, marks):
        area = view(part, marks)
        return push(area, area, shifted(me, "c", 1), (core_send, core_recv), part * 4 + number)

    def unfold(part, core, marks):
        first, width = gather_parts(n)[part]
        free = [axis for axis in "yxz" if marks[axis] is None]

        def one(t, carry):
            at = {**marks, free[0]: t // RING, free[1]: lax.rem(t, RING), "c": core}
            piece = gat_ref[core, at["y"], at["x"], at["z"], :, first:first + width].astype(jnp.float32)
            piece = jnp.where(valid[:, first:first + width], piece * LOG2E, -1e9)
            line = pl.multiple_of(block_of(at) * rows, rows)
            for h in range(HEADS):
                bias_ref[h, pl.ds(line, rows), first:first + width] = piece[h * rows:(h + 1) * rows]
            return carry

        lax.fori_loop(0, RING * RING, one, 0)

    sibling = shifted(me, "c", 1)["c"]
    pending = {}
    shared = {}
    sets = {}
    for phase in range(3):
        marks = {}
        for part, order in enumerate(ORDERS):
            axis = order[phase]
            marks[part] = {a: (None if a in order[:phase] else me[a]) for a in "yxz"}
            if phase > 0:
                for copy in pending[part]:
                    copy.wait_recv()
            pending[part] = []
            if phase < 2:
                area = view(part, marks[part])
                for number, by in enumerate((1, -1, 2)):
                    pending[part].append(
                        push(area, area, shifted(me, axis, by), (send, recv), (part * 3 + phase) * 6 + number)
                    )
                continue
            for kind in range(2):
                for way, by in enumerate((1, -1)):
                    area = view(part, marks[part], half=kind ^ way, split=order[0])
                    number = ((part * 3 + phase) * 3 + kind) * 2 + way
                    pending[part].append(push(area, area, shifted(me, axis, by), (send, recv), number))
            if phase == 2:
                shared[part, 0] = share(part, 0, marks[part])
                sets[part, 0] = marks[part]
        if phase == 2:
            if first_module:
                keep_w.wait()
                w_copy.wait_recv()
            for i in range(4):
                project(i)
            for part in range(3):
                unfold(part, me["c"], sets[part, 0])
        if phase < 2:
            continue
        for part, order in enumerate(ORDERS):
            axis = order[phase]
            split = order[0]
            back = {**marks[part], axis: shifted(me, axis, -1)[axis]}
            ahead = {**marks[part], axis: shifted(me, axis, 1)[axis]}
            later_copies = []
            for way, (by, held) in enumerate(((1, back), (-1, ahead))):
                pending[part][way].wait_recv()
                area = view(part, held, half=way, split=split)
                later_copies.append(
                    push(area, area, shifted(me, axis, by), (send, recv), ((part * 3 + phase) * 3 + 2) * 2 + way)
                )
            sets[part, 1], sets[part, 2] = back, ahead
            pending[part] = pending[part][2:] + later_copies
        if phase == 2:
            for part in range(3):
                for copy in pending[part][:2]:
                    copy.wait_recv()
                pending[part] = pending[part][2:]
                for number in (1, 2):
                    shared[part, number] = share(part, number, sets[part, number])
    for i in range(4, rows):
        project(i)
    if not first_module:
        more.wait_recv()
        norm_row(rows)
        project(rows)
    for part in range(3):
        for number in (1, 2):
            unfold(part, me["c"], sets[part, number])
        shared[part, 0].wait_recv()
        unfold(part, sibling, sets[part, 0])
    vt_ref[:, :, DH:, :] = jnp.ones((*vt_ref.shape[:2], 16, n), jnp.bfloat16)
    for part, order in enumerate(ORDERS):
        for copy in pending[part]:
            copy.wait_recv()
        axis = order[2]
        sets[part, 3] = {**{a: None for a in "yxz"}, axis: shifted(me, axis, 2)[axis]}
        shared[part, 3] = share(part, 3, sets[part, 3])
    for part in range(3):
        unfold(part, me["c"], sets[part, 3])
        for number in (1, 2):
            shared[part, number].wait_recv()
            unfold(part, sibling, sets[part, number])
    for part in range(3):
        shared[part, 3].wait_recv()
        unfold(part, sibling, sets[part, 3])
    for copy in started:
        copy.wait_send()
    if first_module:
        give_w = pltpu.make_async_copy(w_ref.at[1], w_out, local_sem.at[0])
        give_w.start()

    def flip(h, carry):
        side = 128
        for a in range(n // side):
            for b in range(a, n // side):
                rows_a, rows_b = slice(a * side, (a + 1) * side), slice(b * side, (b + 1) * side)
                upper = bias_ref[h, rows_a, rows_b]
                if a < b:
                    lower = bias_ref[h, rows_b, rows_a]
                    bias_ref[h, rows_a, rows_b] = lower.T
                bias_ref[h, rows_b, rows_a] = upper.T
        return carry

    lax.fori_loop(0, HEADS, flip, 0)

    tile = n // TILES

    def away(row):
        return (row // rows) * ((1 - 2 * rep) * rows - 1)

    def row_ends(row, off):
        return stage_ref.at[row, pl.ds(off, span)], out_ref.at[rep * rows + row + away(row), pl.ds(off, span)]

    def row_keep(row, off):
        source, goal = row_ends(row, off)
        return pltpu.make_async_copy(source, goal, row_local.at[row * 2 + off // span])

    def row_give(row, off):
        source, goal = row_ends(row, off)
        number = row * 2 + off // span
        return pltpu.make_async_remote_copy(
            src_ref=source, dst_ref=goal, send_sem=row_send.at[number], recv_sem=row_recv.at[number],
            device_id=device_of(peer), device_id_type=MESH,
        )

    def run(units):
        for slot, row, _, h in units:
            vt_ref[slot, h, :DH, :] = v_ref[row, h * DH:(h + 1) * DH, :]

        def score(unit, t):
            _, row, off, h = units[unit]
            keys = slice(t * tile, (t + 1) * tile)
            queries = q_ref[row, :, pl.ds(off, span)]
            own = jnp.where(owner == h, queries, jnp.zeros_like(queries))
            scores = jnp.dot(k_ref[row, keys, :], own, preferred_element_type=jnp.float32)
            scores = scores + bias_ref[h, keys, pl.ds(off, span)]
            top = jnp.max(scores, axis=0, keepdims=True)
            top_ref[unit % 2] = top if t == 0 else jnp.maximum(top, top_ref[unit % 2])
            score_ref[unit % 2, keys, :] = scores

        def soften(unit, t):
            for first in range(t * tile, (t + 1) * tile, GRAIN):
                keys = slice(first, first + GRAIN)
                expo = jnp.exp2(score_ref[unit % 2, keys, :] - top_ref[unit % 2])
                expo_ref[unit % 2, keys, :] = expo.astype(jnp.bfloat16)

        def combine(unit, t):
            slot, _, _, h = units[unit]
            some = slice(t * (span // TILES), (t + 1) * (span // TILES))
            result = jnp.dot(vt_ref[slot, h], expo_ref[unit % 2, :, some], preferred_element_type=jnp.float32)
            head_ref[h * DH:(h + 1) * DH, some] = result[:DH] / result[DH:DH + 1]

        def finish(slot, row, off, _):
            inside = (row0 + row + away(row)).astype(jnp.float32) < length
            gated = (head_ref[...] * g_ref[row, :, pl.ds(off, span)]).astype(jnp.bfloat16)
            update = lax.dot_general(
                gated, outw_ref[...], (((0,), (0,)), ((), ())), preferred_element_type=jnp.float32
            )
            base = base_ref[row, pl.ds(off, span), :].astype(jnp.float32)
            number = (off + lax.broadcasted_iota(jnp.int32, (span, 1), 0)).astype(jnp.float32)
            result = jnp.where((number < length) & inside, base + update, base)
            if first_module:
                done_ref[slot] = result
            else:
                stage_ref[row, off:off + span, :] = result.astype(jnp.bfloat16)
                row_keep(row, off).start()

                @pl.when(row < rows - 1)
                def _():
                    row_give(row, off).start()

        for stage in range(len(units) + 2):
            for t in range(TILES):
                if stage < len(units):
                    score(stage, t)
                if stage >= 2:
                    combine(stage - 2, t)
                if 1 <= stage <= len(units):
                    soften(stage - 1, t)
            if stage >= 2 and units[stage - 2][3] == HEADS - 1:
                finish(*units[stage - 2])

    if not first_module:
        def each_row(row, carry):
            run([(0, row, off, h) for off in (0, span) for h in range(HEADS)])
            return carry

        lax.fori_loop(0, rows + 1, each_row, 0)
        for row in range(rows + 1):
            for off in (0, span):
                row_keep(row, off).wait()
                if row < rows - 1:
                    row_give(row, off).wait()
        return

    mine_yc = lax.rem(me["y"], 2) * 4 + me["c"] * 2 + me["y"] // 2
    mine_xz = me["x"] * RING + me["z"]

    def first_copy(p, dy, dc):
        at = {**me, "y": lax.rem(me["y"] + dy, RING), "c": lax.rem(me["c"] + dc, CORES)}
        source = stage_ref.at[p, lax.rem(at["y"], 2), :, at["c"] * 2 + at["y"] // 2]
        goal = mail_ref.at[p, mine_yc]
        if dc == 0 and isinstance(dy, int) and dy == 0:
            return pltpu.make_async_copy(source, goal, row_local.at[p])
        number = (p * RING + dy) * CORES + dc
        return pltpu.make_async_remote_copy(
            src_ref=source, dst_ref=goal, send_sem=row_send.at[number], recv_sem=row_recv.at[number],
            device_id=device_of(at), device_id_type=MESH,
        )

    def second_copy(p, k):
        at = level[k]
        source = mail_ref.at[p, :, at["x"] * RING + at["z"]]
        goal = out_ref.at[p, mine_xz]
        if k == 0:
            return pltpu.make_async_copy(source, goal, far_local.at[p])
        number = p * RING * RING + k
        return pltpu.make_async_remote_copy(
            src_ref=source, dst_ref=goal, send_sem=far_send.at[number], recv_sem=far_recv.at[number],
            device_id=device_of(at), device_id_type=MESH,
        )

    def pass_on(p):
        first_copy(p, 0, 0).wait()
        for k in range(1, CORES * RING):
            first_copy(p, k // CORES, k % CORES).wait_recv()
        for k in range(RING * RING):
            second_copy(p, k).start()

    def each_pair(pair, carry):
        def each_span(side, inner):
            off = pl.multiple_of(side * span, span)
            run([(i, pair * 2 + i, off, h) for i in range(2) for h in range(HEADS)])
            both = [done_ref[i].reshape(span // rows, rows, -1) for i in range(2)]
            stage_ref[pair, side] = jnp.concatenate(both, axis=1).astype(jnp.bfloat16).reshape(stage_ref.shape[2:])
            odd = lax.rem(side + me["y"], 2)

            @pl.when(odd == 0)
            def _():
                first_copy(pair, 0, 0).start()

            @pl.when(odd == 1)
            def _():
                first_copy(pair, 1, 0).start()

            first_copy(pair, odd, 1).start()
            first_copy(pair, odd + 2, 0).start()
            first_copy(pair, odd + 2, 1).start()
            return inner

        lax.fori_loop(0, 2, each_span, 0)

        @pl.when(pair > 0)
        def _():
            pass_on(pair - 1)

        return carry

    lax.fori_loop(0, steps, each_pair, 0)
    pass_on(steps - 1)
    for p in range(steps):
        for k in range(1, CORES * RING):
            first_copy(p, k // CORES, k % CORES).wait_send()
        second_copy(p, 0).wait()
        for k in range(1, RING * RING):
            second_copy(p, k).wait_send()
            second_copy(p, k).wait_recv()
    give_w.wait()


def module(source, mask, gain, w, bw, outw, *, first_module, n, rows, ident):
    c = source.shape[-1]
    steps = rows // 2
    yc, xz = CORES * RING, RING * RING
    span = n // 2
    held = rows if first_module else rows + 1
    dma = pltpu.SemaphoreType.DMA
    scratch = [
        pltpu.VMEM((CORES, RING, RING, RING, HEADS * rows, n), jnp.bfloat16),
        pltpu.VMEM((HEADS, n, n), jnp.float32),
        pltpu.VMEM((held, n, c), jnp.bfloat16),
        pltpu.VMEM((held, W, n), jnp.bfloat16),
        pltpu.VMEM((held, n, W), jnp.bfloat16),
        pltpu.VMEM((held, W, n), jnp.bfloat16),
        pltpu.VMEM((held, W, n), jnp.float32),
        pltpu.VMEM((2 if first_module else 1, HEADS, DH + 16, n), jnp.bfloat16),
        pltpu.VMEM((2, n, span), jnp.float32),
        pltpu.VMEM((2, n, span), jnp.bfloat16),
        pltpu.VMEM((W, span), jnp.float32),
        pltpu.VMEM((2, 1, span), jnp.float32),
        pltpu.VMEM((held, n, c), jnp.bfloat16),
        pltpu.VMEM((HEADS * rows, n), jnp.float32),
        pltpu.VMEM((steps, 2, xz, yc // 2, 2 * rows, c) if first_module else (held, n, c), jnp.bfloat16),
        dma((12,)), dma((12,)), dma((54,)), dma((54,)), dma((2,)),
    ]
    vmem = pl.BlockSpec(memory_space=pltpu.VMEM)
    hbm = pl.BlockSpec(memory_space=pl.ANY)
    if first_module:
        out_shape = [
            jax.ShapeDtypeStruct((steps, xz, yc, 2 * rows, c), jnp.bfloat16),
            jax.ShapeDtypeStruct((4, W, c), jnp.bfloat16),
            jax.ShapeDtypeStruct(bw.shape[1:], jnp.bfloat16),
        ]
        out_specs = [hbm, hbm, vmem]
        scratch += [
            dma((steps * yc,)), dma((steps * yc,)), dma((steps,)),
            pltpu.VMEM((2, span, c), jnp.float32),
            pltpu.VMEM((steps, yc, xz, 2 * rows, c), jnp.bfloat16),
            dma((steps * xz,)), dma((steps * xz,)), dma((steps,)),
            pltpu.VMEM((2, 4, W, c), jnp.bfloat16),
            pltpu.VMEM(bw.shape, jnp.bfloat16),
            dma((2,)), dma((2,)),
        ]
    else:
        out_shape = jax.ShapeDtypeStruct((2 * rows, n, c), jnp.bfloat16)
        out_specs = hbm
        scratch += [dma((2 * held,)), dma((2 * held,)), dma((2 * held,)), dma((1,)), dma((1,))]
    return pl.pallas_call(
        functools.partial(module_kernel, first_module=first_module, n=n, rows=rows),
        out_shape=out_shape,
        in_specs=[hbm if first_module else vmem] + [vmem] * 5,
        out_specs=out_specs,
        scratch_shapes=scratch,
        compiler_params=pltpu.CompilerParams(
            collective_id=ident, has_side_effects=True, vmem_limit_bytes=VMEM_LIMIT
        ),
    )(source, mask, gain, w, bw, outw)


def on_device(pair_map, residue_mask, gain_start, proj_start, bias_start, out_start, gain_end, proj_end, bias_end, out_end):
    n = pair_map.shape[1]
    rows = pair_map.shape[0] // 2
    rep = lax.axis_index("rep")
    mask = residue_mask[None, :]
    half = jnp.transpose(jnp.stack([proj_start, proj_end]), (0, 1, 3, 2))
    strip = jnp.transpose(jnp.stack([bias_start, bias_end]), (0, 2, 1))
    strip = lax.dynamic_update_slice_in_dim(
        jnp.zeros((2, 16, strip.shape[2]), strip.dtype), strip, rep * strip.shape[1], 1
    )
    inbox, w_end, strip_end = module(
        pair_map, mask, gain_start[None, :], half, strip, out_start, first_module=True, n=n, rows=rows, ident=0
    )
    return module(
        inbox, mask, gain_end[None, :], w_end, strip_end, out_end, first_module=False, n=n, rows=rows, ident=1
    )


def solution(mesh):
    in_specs = (
        P("dap", None, None), P(), P(), P(None, None, "rep"), P(None, "rep"), P(),
        P(), P(None, None, "rep"), P(None, "rep"), P(),
    )
    return jax.shard_map(on_device, mesh=mesh, in_specs=in_specs, out_specs=P("dap", None, None), check_vma=False)
```

```python
import functools
import math

import jax
import jax.numpy as jnp
from jax import lax
from jax.experimental import pallas as pl
from jax.experimental.pallas import tpu as pltpu
from jax.sharding import PartitionSpec as P

EPS = 1e-5
LOG2E = math.log2(math.e)
HEADS = 4
DH = 32
W = HEADS * DH
VMEM_LIMIT = 60 * 2**20
RING = 4
CORES = 2
MESH = pl.DeviceIdType.MESH


def place():
    dap, rep = lax.axis_index("dap"), lax.axis_index("rep")
    core = lax.rem(dap, CORES)
    z = lax.rem(dap // CORES, RING)
    x = lax.rem(dap // (CORES * RING), RING)
    y = rep * 2 + dap // (CORES * RING * RING)
    return {"c": core, "y": y, "x": x, "z": z}


def block_of(at):
    dap = ((lax.rem(at["y"], 2) * RING + at["x"]) * RING + at["z"]) * CORES + at["c"]
    return dap * 2 + at["y"] // 2


def device_of(at):
    dap = ((lax.rem(at["y"], 2) * RING + at["x"]) * RING + at["z"]) * CORES + at["c"]
    return {"dap": dap, "rep": at["y"] // 2}


def shifted(at, axis, by):
    size = CORES if axis == "c" else RING
    return {**at, axis: lax.rem(at[axis] + by + size, size)}


def normalize(floats, gain):
    center = jnp.mean(floats, axis=-1, keepdims=True)
    apart = floats - center
    spread = jnp.mean(apart * apart, axis=-1, keepdims=True)
    return (apart * lax.rsqrt(spread + EPS) * gain).astype(jnp.bfloat16)


ORDERS = ("xyz", "yzx", "zxy")
GRAIN = 64
TILES = 2


def gather_parts(n):
    unit = n // 8
    return ((0, 3 * unit), (3 * unit, 3 * unit), (6 * unit, 2 * unit))


def module_kernel(*refs, first_module, n, rows):
    if first_module:
        (map_ref, mask_ref, gain_ref, half_ref, strip_ref, outw_ref, out_ref, w_out, bw_out) = refs[:9]
        (gat_ref, bias_ref, norm_ref, q_ref, k_ref, v_ref, g_ref, vt_ref, score_ref, expo_ref, head_ref, top_ref, base_ref,
         own32, stage_ref, core_send, core_recv, send, recv, local_sem, row_send, row_recv, row_local,
         done_ref, mail_ref, far_send, far_recv, far_local, w_ref, strip_in, w_send, w_recv) = refs[9:]
    else:
        (map_ref, mask_ref, gain_ref, w_ref, bw_ref, outw_ref, out_ref) = refs[:7]
        (gat_ref, bias_ref, norm_ref, q_ref, k_ref, v_ref, g_ref, vt_ref, score_ref, expo_ref, head_ref, top_ref, base_ref,
         own32, stage_ref, core_send, core_recv, send, recv, local_sem, row_send, row_recv, row_local, more_send, more_recv) = refs[7:]
    me = place()
    rep = lax.axis_index("rep")
    peer = shifted(me, "y", 2)
    row0 = block_of(me) * rows
    steps = rows // 2
    span = n // 2
    column = [{**me, "y": lax.rem(me["y"] + k // CORES, RING), "c": lax.rem(me["c"] + k % CORES, CORES)}
              for k in range(CORES * RING)]
    level = [{**me, "x": lax.rem(me["x"] + k // RING, RING), "z": lax.rem(me["z"] + k % RING, RING)}
             for k in range(RING * RING)]
    owner = lax.broadcasted_iota(jnp.int32, (W, 1), 0) // DH
    mask = mask_ref[...].astype(jnp.float32)
    length = jnp.sum(mask, axis=1, keepdims=True)
    valid = mask > 0.5

    if first_module:
        partners = column[1:] + level[1:]
    else:
        partners = [shifted(me, axis, by) for axis in "xyz" for by in (1, -1, 2)] + [shifted(me, "c", 1)]
    barrier = pltpu.get_barrier_semaphore()
    for partner in partners:
        pl.semaphore_signal(barrier, inc=1, device_id=device_of(partner), device_id_type=MESH)

    started = []

    def push(src, dst, to, semaphores, number):
        copy = pltpu.make_async_remote_copy(
            src_ref=src, dst_ref=dst, send_sem=semaphores[0].at[number], recv_sem=semaphores[1].at[number],
            device_id=device_of(to), device_id_type=MESH,
        )
        copy.start()
        started.append(copy)
        return copy

    if first_module:
        fetch = pltpu.make_async_copy(map_ref.at[pl.ds(rep * rows, rows)], base_ref, local_sem.at[0])
        fetch.start()
        place_w = w_ref.at[:, :, pl.ds(rep * (W // 2), W // 2), :]
        keep_w = pltpu.make_async_copy(half_ref, place_w, local_sem.at[1])
        keep_w.start()
        pl.semaphore_wait(barrier, len(partners))
        strip_copy = push(strip_ref, strip_in, peer, (w_send, w_recv), 0)
        w_copy = push(half_ref, place_w, peer, (w_send, w_recv), 1)
        fetch.wait()
    else:
        four = 4 * rows * rows
        to = lax.broadcasted_iota(jnp.int32, (four, four), 0)
        come = lax.broadcasted_iota(jnp.int32, (four, four), 1)
        j, which, i = to // (4 * rows), (to // rows) % 4, to % rows
        turn = (come == ((i // 2 * 4 + which) * 2 + i % 2) * rows + j).astype(jnp.bfloat16)
        pl.semaphore_wait(barrier, len(partners))

    def norm_row(i):
        norm_ref[i] = normalize(base_ref[i].astype(jnp.float32), gain_ref[...])

    def make_part(part):
        first, width = gather_parts(n)[part]
        here = slice(first, first + width)
        if not first_module:
            for group in range(first // (4 * rows), (first + width) // (4 * rows)):
                low, xz = group // (RING * RING), group % (RING * RING)
                piece = map_ref[:, xz, 4 * low:4 * low + 4].reshape(four, -1)
                result = jnp.dot(turn, piece, preferred_element_type=jnp.float32)
                base_ref[:rows, group * 4 * rows:(group + 1) * 4 * rows, :] = (
                    result.reshape(rows, 4 * rows, -1).astype(jnp.bfloat16)
                )
        for i in range(rows):
            norm_ref[i, here, :] = normalize(base_ref[i, here, :].astype(jnp.float32), gain_ref[...])
        if first_module:
            if part == 0:
                strip_copy.wait_recv()
            weights = strip_ref[0] + strip_in[0]
        else:
            weights = bw_ref[...]
        for i in range(rows):
            strip = lax.dot_general(
                weights, norm_ref[i, here, :], (((1,), (1,)), ((), ())), preferred_element_type=jnp.float32
            )
            for h in range(HEADS):
                own32[h * rows + i:h * rows + i + 1, here] = strip[h:h + 1]
        gat_ref[me["c"], me["y"], me["x"], me["z"], :, here] = own32[:, here].astype(jnp.bfloat16)

    def project(i):
        normed = norm_ref[i]
        weights = w_ref[0] if first_module else w_ref[...]
        both = (((1,), (1,)), ((), ()))
        queries = lax.dot_general(weights[0], normed, both, preferred_element_type=jnp.float32)
        q_ref[i] = (queries * (DH**-0.5 * LOG2E)).astype(jnp.bfloat16)
        rest = lax.dot_general(weights[2:].reshape(2 * W, -1), normed, both, preferred_element_type=jnp.float32)
        v_ref[i] = rest[:W].astype(jnp.bfloat16)
        g_ref[i] = jax.nn.sigmoid(rest[W:])
        k_ref[i] = lax.dot_general(normed, weights[1], both, preferred_element_type=jnp.float32).astype(jnp.bfloat16)

    def view(part, marks, half=None, split=None):
        first, width = gather_parts(n)[part]
        index = [me["c"]]
        for axis in "yxz":
            mark = marks[axis]
            if axis == split:
                index.append(pl.ds(2 * half, 2))
            elif mark is None:
                index.append(slice(None))
            else:
                index.append(mark)
        lines = pl.ds(16 * half, 16) if half is not None and split is None else slice(None)
        return gat_ref.at[(*index, lines, pl.ds(first, width))]

    def share(part, number, marks):
        area = view(part, marks)
        return push(area, area, shifted(me, "c", 1), (core_send, core_recv), part * 4 + number)

    def unfold(part, core, marks):
        first, width = gather_parts(n)[part]
        free = [axis for axis in "yxz" if marks[axis] is None]

        def one(t, carry):
            at = {**marks, free[0]: t // RING, free[1]: lax.rem(t, RING), "c": core}
            piece = gat_ref[core, at["y"], at["x"], at["z"], :, first:first + width].astype(jnp.float32)
            piece = jnp.where(valid[:, first:first + width], piece * LOG2E, -1e9)
            line = pl.multiple_of(block_of(at) * rows, rows)
            for h in range(HEADS):
                bias_ref[h, pl.ds(line, rows), first:first + width] = piece[h * rows:(h + 1) * rows]
            return carry

        lax.fori_loop(0, RING * RING, one, 0)

    sibling = shifted(me, "c", 1)["c"]
    pending = {}
    shared = {}
    sets = {}
    for phase in range(3):
        marks = {}
        for part, order in enumerate(ORDERS):
            axis = order[phase]
            marks[part] = {a: (None if a in order[:phase] else me[a]) for a in "yxz"}
            if phase > 0:
                for copy in pending[part]:
                    copy.wait_recv()
            pending[part] = []
            if phase == 0:
                make_part(part)
            if phase < 2:
                area = view(part, marks[part])
                for number, by in enumerate((1, -1, 2)):
                    pending[part].append(
                        push(area, area, shifted(me, axis, by), (send, recv), (part * 3 + phase) * 6 + number)
                    )
                continue
            for kind in range(2):
                for way, by in enumerate((1, -1)):
                    area = view(part, marks[part], half=kind ^ way, split=order[0])
                    number = ((part * 3 + phase) * 3 + kind) * 2 + way
                    pending[part].append(push(area, area, shifted(me, axis, by), (send, recv), number))
            if phase == 2:
                shared[part, 0] = share(part, 0, marks[part])
                sets[part, 0] = marks[part]
        if phase == 2:
            if first_module:
                keep_w.wait()
                w_copy.wait_recv()
            for i in range(4):
                project(i)
            for part in range(3):
                unfold(part, me["c"], sets[part, 0])
        if phase == 0 and first_module:
            bw_out[...] = strip_ref[1] + strip_in[1]
        elif phase == 0:
            more = push(base_ref.at[rows - 1], base_ref.at[rows], peer, (more_send, more_recv), 0)
        if phase < 2:
            continue
        for part, order in enumerate(ORDERS):
            axis = order[phase]
            split = order[0]
            back = {**marks[part], axis: shifted(me, axis, -1)[axis]}
            ahead = {**marks[part], axis: shifted(me, axis, 1)[axis]}
            later_copies = []
            for way, (by, held) in enumerate(((1, back), (-1, ahead))):
                pending[part][way].wait_recv()
                area = view(part, held, half=way, split=split)
                later_copies.append(
                    push(area, area, shifted(me, axis, by), (send, recv), ((part * 3 + phase) * 3 + 2) * 2 + way)
                )
            sets[part, 1], sets[part, 2] = back, ahead
            pending[part] = pending[part][2:] + later_copies
        if phase == 2:
            for part in range(3):
                for copy in pending[part][:2]:
                    copy.wait_recv()
                pending[part] = pending[part][2:]
                for number in (1, 2):
                    shared[part, number] = share(part, number, sets[part, number])
    for i in range(4, rows):
        project(i)
    if not first_module:
        more.wait_recv()
        norm_row(rows)
        project(rows)
    for part in range(3):
        for number in (1, 2):
            unfold(part, me["c"], sets[part, number])
        shared[part, 0].wait_recv()
        unfold(part, sibling, sets[part, 0])
    vt_ref[:, :, DH:, :] = jnp.ones((*vt_ref.shape[:2], 16, n), jnp.bfloat16)
    for part, order in enumerate(ORDERS):
        for copy in pending[part]:
            copy.wait_recv()
        axis = order[2]
        sets[part, 3] = {**{a: None for a in "yxz"}, axis: shifted(me, axis, 2)[axis]}
        shared[part, 3] = share(part, 3, sets[part, 3])
    for part in range(3):
        unfold(part, me["c"], sets[part, 3])
        for number in (1, 2):
            shared[part, number].wait_recv()
            unfold(part, sibling, sets[part, number])
    for part in range(3):
        shared[part, 3].wait_recv()
        unfold(part, sibling, sets[part, 3])
    for copy in started:
        copy.wait_send()
    if first_module:
        give_w = pltpu.make_async_copy(w_ref.at[1], w_out, local_sem.at[0])
        give_w.start()

    def flip(h, carry):
        side = 128
        for a in range(n // side):
            for b in range(a, n // side):
                rows_a, rows_b = slice(a * side, (a + 1) * side), slice(b * side, (b + 1) * side)
                upper = bias_ref[h, rows_a, rows_b]
                if a < b:
                    lower = bias_ref[h, rows_b, rows_a]
                    bias_ref[h, rows_a, rows_b] = lower.T
                bias_ref[h, rows_b, rows_a] = upper.T
        return carry

    lax.fori_loop(0, HEADS, flip, 0)

    tile = n // TILES

    def away(row):
        return (row // rows) * ((1 - 2 * rep) * rows - 1)

    def row_ends(row, off):
        return stage_ref.at[row, pl.ds(off, span)], out_ref.at[rep * rows + row + away(row), pl.ds(off, span)]

    def row_keep(row, off):
        source, goal = row_ends(row, off)
        return pltpu.make_async_copy(source, goal, row_local.at[row * 2 + off // span])

    def row_give(row, off):
        source, goal = row_ends(row, off)
        number = row * 2 + off // span
        return pltpu.make_async_remote_copy(
            src_ref=source, dst_ref=goal, send_sem=row_send.at[number], recv_sem=row_recv.at[number],
            device_id=device_of(peer), device_id_type=MESH,
        )

    def run(units):
        for slot, row, _, h in units:
            vt_ref[slot, h, :DH, :] = v_ref[row, h * DH:(h + 1) * DH, :]

        def score(unit, t):
            _, row, off, h = units[unit]
            keys = slice(t * tile, (t + 1) * tile)
            queries = q_ref[row, :, pl.ds(off, span)]
            own = jnp.where(owner == h, queries, jnp.zeros_like(queries))
            scores = jnp.dot(k_ref[row, keys, :], own, preferred_element_type=jnp.float32)
            scores = scores + bias_ref[h, keys, pl.ds(off, span)]
            top = jnp.max(scores, axis=0, keepdims=True)
            top_ref[unit % 2] = top if t == 0 else jnp.maximum(top, top_ref[unit % 2])
            score_ref[unit % 2, keys, :] = scores

        def soften(unit, t):
            for first in range(t * tile, (t + 1) * tile, GRAIN):
                keys = slice(first, first + GRAIN)
                expo = jnp.exp2(score_ref[unit % 2, keys, :] - top_ref[unit % 2])
                expo_ref[unit % 2, keys, :] = expo.astype(jnp.bfloat16)

        def combine(unit, t):
            slot, _, _, h = units[unit]
            some = slice(t * (span // TILES), (t + 1) * (span // TILES))
            result = jnp.dot(vt_ref[slot, h], expo_ref[unit % 2, :, some], preferred_element_type=jnp.float32)
            head_ref[h * DH:(h + 1) * DH, some] = result[:DH] / result[DH:DH + 1]

        def finish(slot, row, off, _):
            inside = (row0 + row + away(row)).astype(jnp.float32) < length
            gated = (head_ref[...] * g_ref[row, :, pl.ds(off, span)]).astype(jnp.bfloat16)
            update = lax.dot_general(
                gated, outw_ref[...], (((0,), (0,)), ((), ())), preferred_element_type=jnp.float32
            )
            base = base_ref[row, pl.ds(off, span), :].astype(jnp.float32)
            number = (off + lax.broadcasted_iota(jnp.int32, (span, 1), 0)).astype(jnp.float32)
            result = jnp.where((number < length) & inside, base + update, base)
            if first_module:
                done_ref[slot] = result
            else:
                stage_ref[row, off:off + span, :] = result.astype(jnp.bfloat16)
                row_keep(row, off).start()

                @pl.when(row < rows - 1)
                def _():
                    row_give(row, off).start()

        for stage in range(len(units) + 2):
            for t in range(TILES):
                if stage < len(units):
                    score(stage, t)
                if stage >= 2:
                    combine(stage - 2, t)
                if 1 <= stage <= len(units):
                    soften(stage - 1, t)
            if stage >= 2 and units[stage - 2][3] == HEADS - 1:
                finish(*units[stage - 2])

    if not first_module:
        def each_row(row, carry):
            run([(0, row, off, h) for off in (0, span) for h in range(HEADS)])
            return carry

        lax.fori_loop(0, rows + 1, each_row, 0)
        for row in range(rows + 1):
            for off in (0, span):
                row_keep(row, off).wait()
                if row < rows - 1:
                    row_give(row, off).wait()
        return

    mine_yc = lax.rem(me["y"], 2) * 4 + me["c"] * 2 + me["y"] // 2
    mine_xz = me["x"] * RING + me["z"]

    def first_copy(p, dy, dc):
        at = {**me, "y": lax.rem(me["y"] + dy, RING), "c": lax.rem(me["c"] + dc, CORES)}
        source = stage_ref.at[p, lax.rem(at["y"], 2), :, at["c"] * 2 + at["y"] // 2]
        goal = mail_ref.at[p, mine_yc]
        if dc == 0 and isinstance(dy, int) and dy == 0:
            return pltpu.make_async_copy(source, goal, row_local.at[p])
        number = (p * RING + dy) * CORES + dc
        return pltpu.make_async_remote_copy(
            src_ref=source, dst_ref=goal, send_sem=row_send.at[number], recv_sem=row_recv.at[number],
            device_id=device_of(at), device_id_type=MESH,
        )

    def second_copy(p, k):
        at = level[k]
        source = mail_ref.at[p, :, at["x"] * RING + at["z"]]
        goal = out_ref.at[p, mine_xz]
        if k == 0:
            return pltpu.make_async_copy(source, goal, far_local.at[p])
        number = p * RING * RING + k
        return pltpu.make_async_remote_copy(
            src_ref=source, dst_ref=goal, send_sem=far_send.at[number], recv_sem=far_recv.at[number],
            device_id=device_of(at), device_id_type=MESH,
        )

    def pass_on(p):
        first_copy(p, 0, 0).wait()
        for k in range(1, CORES * RING):
            first_copy(p, k // CORES, k % CORES).wait_recv()
        for k in range(RING * RING):
            second_copy(p, k).start()

    def each_pair(pair, carry):
        def each_span(side, inner):
            off = pl.multiple_of(side * span, span)
            run([(i, pair * 2 + i, off, h) for i in range(2) for h in range(HEADS)])
            both = [done_ref[i].reshape(span // rows, rows, -1) for i in range(2)]
            stage_ref[pair, side] = jnp.concatenate(both, axis=1).astype(jnp.bfloat16).reshape(stage_ref.shape[2:])
            odd = lax.rem(side + me["y"], 2)

            @pl.when(odd == 0)
            def _():
                first_copy(pair, 0, 0).start()

            @pl.when(odd == 1)
            def _():
                first_copy(pair, 1, 0).start()

            first_copy(pair, odd, 1).start()
            first_copy(pair, odd + 2, 0).start()
            first_copy(pair, odd + 2, 1).start()
            return inner

        lax.fori_loop(0, 2, each_span, 0)

        @pl.when(pair > 0)
        def _():
            pass_on(pair - 1)

        return carry

    lax.fori_loop(0, steps, each_pair, 0)
    pass_on(steps - 1)
    for p in range(steps):
        for k in range(1, CORES * RING):
            first_copy(p, k // CORES, k % CORES).wait_send()
        second_copy(p, 0).wait()
        for k in range(1, RING * RING):
            second_copy(p, k).wait_send()
            second_copy(p, k).wait_recv()
    give_w.wait()


def module(source, mask, gain, w, bw, outw, *, first_module, n, rows, ident):
    c = source.shape[-1]
    steps = rows // 2
    yc, xz = CORES * RING, RING * RING
    span = n // 2
    held = rows if first_module else rows + 1
    dma = pltpu.SemaphoreType.DMA
    scratch = [
        pltpu.VMEM((CORES, RING, RING, RING, HEADS * rows, n), jnp.bfloat16),
        pltpu.VMEM((HEADS, n, n), jnp.float32),
        pltpu.VMEM((held, n, c), jnp.bfloat16),
        pltpu.VMEM((held, W, n), jnp.bfloat16),
        pltpu.VMEM((held, n, W), jnp.bfloat16),
        pltpu.VMEM((held, W, n), jnp.bfloat16),
        pltpu.VMEM((held, W, n), jnp.float32),
        pltpu.VMEM((2 if first_module else 1, HEADS, DH + 16, n), jnp.bfloat16),
        pltpu.VMEM((2, n, span), jnp.float32),
        pltpu.VMEM((2, n, span), jnp.bfloat16),
        pltpu.VMEM((W, span), jnp.float32),
        pltpu.VMEM((2, 1, span), jnp.float32),
        pltpu.VMEM((held, n, c), jnp.bfloat16),
        pltpu.VMEM((HEADS * rows, n), jnp.float32),
        pltpu.VMEM((steps, 2, xz, yc // 2, 2 * rows, c) if first_module else (held, n, c), jnp.bfloat16),
        dma((12,)), dma((12,)), dma((54,)), dma((54,)), dma((2,)),
    ]
    vmem = pl.BlockSpec(memory_space=pltpu.VMEM)
    hbm = pl.BlockSpec(memory_space=pl.ANY)
    if first_module:
        out_shape = [
            jax.ShapeDtypeStruct((steps, xz, yc, 2 * rows, c), jnp.bfloat16),
            jax.ShapeDtypeStruct((4, W, c), jnp.bfloat16),
            jax.ShapeDtypeStruct(bw.shape[1:], jnp.bfloat16),
        ]
        out_specs = [hbm, hbm, vmem]
        scratch += [
            dma((steps * yc,)), dma((steps * yc,)), dma((steps,)),
            pltpu.VMEM((2, span, c), jnp.float32),
            pltpu.VMEM((steps, yc, xz, 2 * rows, c), jnp.bfloat16),
            dma((steps * xz,)), dma((steps * xz,)), dma((steps,)),
            pltpu.VMEM((2, 4, W, c), jnp.bfloat16),
            pltpu.VMEM(bw.shape, jnp.bfloat16),
            dma((2,)), dma((2,)),
        ]
    else:
        out_shape = jax.ShapeDtypeStruct((2 * rows, n, c), jnp.bfloat16)
        out_specs = hbm
        scratch += [dma((2 * held,)), dma((2 * held,)), dma((2 * held,)), dma((1,)), dma((1,))]
    return pl.pallas_call(
        functools.partial(module_kernel, first_module=first_module, n=n, rows=rows),
        out_shape=out_shape,
        in_specs=[hbm if first_module else vmem] + [vmem] * 5,
        out_specs=out_specs,
        scratch_shapes=scratch,
        compiler_params=pltpu.CompilerParams(
            collective_id=ident, has_side_effects=True, vmem_limit_bytes=VMEM_LIMIT
        ),
    )(source, mask, gain, w, bw, outw)


def on_device(pair_map, residue_mask, gain_start, proj_start, bias_start, out_start, gain_end, proj_end, bias_end, out_end):
    n = pair_map.shape[1]
    rows = pair_map.shape[0] // 2
    rep = lax.axis_index("rep")
    mask = residue_mask[None, :]
    half = jnp.transpose(jnp.stack([proj_start, proj_end]), (0, 1, 3, 2))
    strip = jnp.transpose(jnp.stack([bias_start, bias_end]), (0, 2, 1))
    strip = lax.dynamic_update_slice_in_dim(
        jnp.zeros((2, 16, strip.shape[2]), strip.dtype), strip, rep * strip.shape[1], 1
    )
    inbox, w_end, strip_end = module(
        pair_map, mask, gain_start[None, :], half, strip, out_start, first_module=True, n=n, rows=rows, ident=0
    )
    return module(
        inbox, mask, gain_end[None, :], w_end, strip_end, out_end, first_module=False, n=n, rows=rows, ident=1
    )


def solution(mesh):
    in_specs = (
        P("dap", None, None), P(), P(), P(None, None, "rep"), P(None, "rep"), P(),
        P(), P(None, None, "rep"), P(None, "rep"), P(),
    )
    return jax.shard_map(on_device, mesh=mesh, in_specs=in_specs, out_specs=P("dap", None, None), check_vma=False)
```
